128 devices in a mesh: seq: 8 (over z, core), vocab: 16 (over y, x).
Axes of the slice: x: 4, y: 4, z: 4, core: 2. Of those that a mesh axis runs over, the one named last changes fastest.
Arguments:
- hidden: bfloat16 [512, 5376], P('seq', 'vocab'), may hold values from -48 to 48
- head_weight: bfloat16 [131072, 5376], P(('seq', 'vocab')), may hold values from -1 to 1
- teacher_logits: float32 [512, 256], P(('seq', 'vocab')), may hold values from -16 to 300
- teacher_ids: int32 [512, 256], P(('seq', 'vocab')), may hold values from 0 to 131071, as said below
Outputs:
- cross_entropy: float32 [512], P(('seq', 'vocab'))
- entropy: float32 [512], P(('seq', 'vocab'))
- grad_hidden: bfloat16 [512, 5376], P('seq', 'vocab')
- grad_weight: bfloat16 [131072, 5376], P(('seq', 'vocab'))
The draws below stay inside these ranges and needn't reach their ends.
Inputs may be any that keep to these rules, and one draw needn't show every extreme that they name: `teacher_ids`: each row names 256 different ids, grouped by owner o = id // 1024 in ascending order of o. In every row one owner has exactly 6 ids, every other owner 1 or 2.
All inputs are finite; a program needn't handle non-finite values.
Results may differ from the reference program's by a relative error of at most 0.011.
Values may be sent and summed in bfloat16 or wider, within the bound.
No kernel may reach another device: no remote copies, remote signals or barrier semaphores. Data moves between devices by JAX's collectives and lax.ppermute only.
A program may use at most 128 MiB of HBM per device.

```python
import jax
import jax.numpy as jnp
from jax import lax

D = 5376
V_DEV = 1024
TEACH = 256
OWNERS = 128
VOCAB = 131072
TOKENS = 512
MOST = 6


def weight_table(key):
    values = jax.random.truncated_normal(key, -4.0, 4.0, (VOCAB, D), jnp.float32) * D ** (-0.5)
    return values.astype(jnp.bfloat16)


def draw_head_weight(key, part):
    return weight_table(key)


def draw_hidden(key, part):
    key = jax.random.fold_in(key, 11)
    values = jax.random.truncated_normal(key, -4.0, 4.0, (TOKENS, D), jnp.float32) * 3.0
    return values.astype(jnp.bfloat16)


def draw_teacher_logits(key, part):
    key = jax.random.fold_in(key, 23)
    return jax.random.truncated_normal(key, -4.0, 4.0, (TOKENS, TEACH), jnp.float32) * 3.0


def draw_teacher_ids(key, part):
    key = jax.random.fold_in(key, 37)
    keys = jax.random.split(key, 5)
    hot_owner = jax.random.randint(keys[0], (TOKENS,), 0, OWNERS) * jax.random.randint(keys[1], (TOKENS,), 0, OWNERS) // OWNERS
    owner_iota = jnp.arange(OWNERS, dtype=jnp.int32)
    is_hot = owner_iota[None, :] == hot_owner[:, None]
    scores = jax.random.randint(keys[2], (TOKENS, OWNERS), 0, 1 << 20) * OWNERS + owner_iota[None, :]
    scores = jnp.where(is_hot, jnp.int32(1 << 30), scores)
    rank_of = jnp.argsort(jnp.argsort(scores, axis=1), axis=1).astype(jnp.int32)
    base_count = (TEACH - MOST) // (OWNERS - 1)
    extra_count = TEACH - MOST - base_count * (OWNERS - 1)
    counts = jnp.where(is_hot, MOST, base_count + (rank_of < extra_count).astype(jnp.int32))
    end_pos = jnp.cumsum(counts, axis=1)
    start_pos = end_pos - counts
    slot_pos = jnp.arange(TEACH, dtype=jnp.int32)
    owner_k = jnp.sum((end_pos[:, None, :] <= slot_pos[None, :, None]).astype(jnp.int32), axis=2)
    within = slot_pos[None, :] - jnp.take_along_axis(start_pos, owner_k, axis=1)
    begin_pos = jax.random.randint(keys[3], (TOKENS, OWNERS), 0, V_DEV)
    begin_pos = begin_pos.at[0, 0].set(0).at[0, OWNERS - 1].set(V_DEV - 1)
    stride = 2 * jax.random.randint(keys[4], (TOKENS, OWNERS), 0, V_DEV // 2) + 1
    local_ids = (jnp.take_along_axis(begin_pos, owner_k, axis=1) + within * jnp.take_along_axis(stride, owner_k, axis=1)) % V_DEV
    return (owner_k * V_DEV + local_ids).astype(jnp.int32)


def setup_inputs(seed: int = 0) -> dict:
    key_list = jax.random.split(jax.random.key(seed), 5)
    hidden = draw_hidden(jax.random.fold_in(key_list[4], 71), 0)
    head_weight = draw_head_weight(jax.random.fold_in(key_list[4], 71), 0)
    teacher_logits = draw_teacher_logits(jax.random.fold_in(key_list[4], 71), 0)
    teacher_ids = draw_teacher_ids(jax.random.fold_in(key_list[4], 71), 0)
    return dict(hidden=hidden, head_weight=head_weight, teacher_logits=teacher_logits, teacher_ids=teacher_ids)


loss_scale = 64.0


def reference(hidden, head_weight, teacher_logits, teacher_ids):
    highest = lax.Precision.HIGHEST
    teacher_prob = jax.nn.softmax(teacher_logits.astype(jnp.float32), axis=1)
    row_ids = jnp.broadcast_to(jnp.arange(TOKENS, dtype=jnp.int32)[:, None], teacher_ids.shape)
    target = jnp.zeros((TOKENS, VOCAB), jnp.float32).at[row_ids, teacher_ids].add(teacher_prob)
    hidden_full = hidden.astype(jnp.float32)
    block_ids = jnp.arange(OWNERS, dtype=jnp.int32)

    def logits_of(block_id):
        weight_block = lax.dynamic_slice_in_dim(head_weight, block_id * V_DEV, V_DEV, 0).astype(jnp.float32)
        target_block = lax.dynamic_slice_in_dim(target, block_id * V_DEV, V_DEV, 1)
        return weight_block, target_block, jnp.dot(hidden_full, weight_block.T, precision=highest)

    def gather_stats(state_carry, block_id):
        peak_val, total_sum, moment, cross_sum = state_carry
        weight_block, target_block, logits = logits_of(block_id)
        new_peak = jnp.maximum(peak_val, jnp.max(logits, axis=1))
        rescale = jnp.exp(peak_val - new_peak)
        expo = jnp.exp(logits - new_peak[:, None])
        return (new_peak, total_sum * rescale + jnp.sum(expo, axis=1),
                moment * rescale + jnp.sum(expo * logits, axis=1),
                cross_sum + jnp.sum(target_block * logits, axis=1)), None

    start_state = (jnp.full((TOKENS,), -jnp.inf, jnp.float32), jnp.zeros((TOKENS,), jnp.float32),
                   jnp.zeros((TOKENS,), jnp.float32), jnp.zeros((TOKENS,), jnp.float32))
    (peak_val, total_sum, moment, cross_sum), _ = lax.scan(gather_stats, start_state, block_ids)
    log_total = peak_val + jnp.log(total_sum)
    cross_entropy = log_total - cross_sum
    entropy = log_total - moment / total_sum

    def gradients(grad_acc, block_id):
        weight_block, target_block, logits = logits_of(block_id)
        student = jnp.exp(logits - peak_val[:, None]) / total_sum[:, None]
        rounded = (loss_scale * (student - target_block)).astype(jnp.bfloat16)
        grad_logits = lax.optimization_barrier(rounded).astype(jnp.float32)
        grad_acc = grad_acc + jnp.dot(grad_logits, weight_block, precision=highest)
        grad_block = jnp.dot(grad_logits.T, hidden_full, precision=highest).astype(jnp.bfloat16)
        return grad_acc, grad_block

    grad_acc, grad_blocks = lax.scan(gradients, jnp.zeros((TOKENS, D), jnp.float32), block_ids)
    return cross_entropy, entropy, grad_acc.astype(jnp.bfloat16), grad_blocks.reshape(VOCAB, D)
```

```python
import functools

import jax
import jax.numpy as jnp
from jax import lax
from jax.experimental import pallas as pl
from jax.experimental.pallas import tpu as pltpu
from jax.sharding import PartitionSpec as P

loss_scale = 64.0
SLOTS = 6
OFFSETS = (0, 3, 1, 2)
LANES = 128
ANY = pl.BlockSpec(memory_space=pl.ANY)
VMEM_LIMIT = 50 * 1024 * 1024
BOTH = ("seq", "vocab")


def params():
    return pltpu.CompilerParams(vmem_limit_bytes=VMEM_LIMIT)


def cost(flops, nbytes):
    return pl.CostEstimate(flops=int(flops), bytes_accessed=int(nbytes), transcendentals=0)


def teacher_kernel(owners, vocab_rows, logits_ref, ids_ref, out_ref):
    rows, width = logits_ref.shape
    scores = logits_ref[...]
    expo = jnp.exp(scores - jnp.max(scores, axis=1, keepdims=True))
    prob = expo / jnp.sum(expo, axis=1, keepdims=True)
    ids = ids_ref[...]
    shift = vocab_rows.bit_length() - 1
    owner_iota = lax.broadcasted_iota(jnp.int32, (owners, width), 0)
    slot_iota = lax.broadcasted_iota(jnp.int32, (owners, width), 1)
    lane = lax.broadcasted_iota(jnp.int32, (owners, rows * 16), 1)
    out = jnp.zeros((owners, rows * 16), jnp.float32)
    for row in range(rows):
        row_ids = jnp.broadcast_to(ids[row : row + 1, :], (owners, width))
        row_prob = jnp.broadcast_to(prob[row : row + 1, :], (owners, width))
        owner = lax.shift_right_logical(row_ids, shift)
        start = jnp.sum((owner < owner_iota).astype(jnp.int32), axis=1, keepdims=True)
        place = jnp.where(owner == owner_iota, slot_iota - start, -1)
        local = (row_ids - owner * vocab_rows + 1).astype(jnp.float32)
        for slot in range(SLOTS):
            hit = place == slot
            value = jnp.sum(jnp.where(hit, row_prob, 0.0), axis=1, keepdims=True)
            index = jnp.sum(jnp.where(hit, local, 0.0), axis=1, keepdims=True) - 1.0
            out = out + jnp.where(lane == row * 16 + slot, value, 0.0)
            out = out + jnp.where(lane == row * 16 + 8 + slot, index, 0.0)
    out_ref[...] = out


def teacher_rows(owners, vocab_rows, teacher_logits, teacher_ids):
    rows = teacher_logits.shape[0]
    return pl.pallas_call(
        functools.partial(teacher_kernel, owners, vocab_rows),
        out_shape=jax.ShapeDtypeStruct((owners, rows * 16), jnp.float32),
        compiler_params=params(),
        cost_estimate=cost(4e6, 40000),
    )(teacher_logits, teacher_ids)


def dot_nt(a, b):
    return lax.dot_general(a, b, (((1,), (1,)), ((), ())), preferred_element_type=jnp.float32)


def local_stats(logits, target):
    peak = jnp.max(logits, axis=0, keepdims=True)
    expo = jnp.exp(logits - peak)
    total = jnp.sum(expo, axis=0, keepdims=True)
    mean = jnp.sum(expo * logits, axis=0, keepdims=True) / total
    cross = jnp.sum(target * logits, axis=0, keepdims=True)
    lse = peak + jnp.log(total)
    row = lax.broadcasted_iota(jnp.int32, (8, LANES), 0)
    return jnp.where(row == 0, lse, jnp.where(row == 1, mean, jnp.where(row == 2, cross, 0.0)))


def load_blocks(pieces, dest, sems):
    copies = [
        pltpu.make_async_copy(src, dest.at[pl.ds(pl.multiple_of(row, 32), src.shape[0])], sems.at[k])
        for k, (src, row) in enumerate(pieces)
    ]
    for copy in copies:
        copy.start()
    return copies


def first_kernel(pos, got, w, own, own2, left, left2, right, right2, out, target, stats, held, keep, teach, sems):
    step = pl.program_id(0)
    z, core = pos[0], pos[1]
    mine, other = core * 64, (1 - core) * 64

    @pl.when(step == 0)
    def _():
        copies = load_blocks(
            [(own, mine), (own2, other), (left, 128 + mine), (left2, 128 + other), (right, 256 + mine), (right2, 256 + other)],
            held, sems,
        )
        flipped = got[...].T
        source = lax.broadcasted_iota(jnp.int32, (LANES, 4 * LANES), 0)
        token = lax.broadcasted_iota(jnp.int32, (LANES, 4 * LANES), 1)
        spread = jnp.zeros((16, 4 * LANES), jnp.float32)
        for row in range(4):
            pick = (token == source * 4 + row).astype(jnp.float32)
            spread = spread + jnp.dot(
                flipped[row * 16 : row * 16 + 16], pick,
                precision=lax.Precision.HIGHEST, preferred_element_type=jnp.float32,
            )
        for block in range(4):
            teach[block] = spread[:, block * LANES : (block + 1) * LANES]
        for copy in copies:
            copy.wait()

    rows = w.shape[0]
    logits = dot_nt(w[...], held[...])
    base = pl.multiple_of(step * rows, rows)
    word = (lax.broadcasted_iota(jnp.int32, (rows, LANES), 0) + step * rows).astype(jnp.float32)
    for slot in range(4):
        info = teach[(z + OFFSETS[slot]) % 4]
        dense = jnp.zeros((rows, LANES), jnp.float32)
        for k in range(SLOTS):
            dense = dense + jnp.where(word == info[8 + k : 9 + k], info[k : k + 1], 0.0)
        target[slot] = dense
        if slot < 3:
            part = logits[:, slot * LANES : (slot + 1) * LANES]
            out[slot] = part
            keep[slot, pl.ds(base, rows)] = part
            keep[3 + slot, pl.ds(base, rows)] = dense

    @pl.when(step == pl.num_programs(0) - 1)
    def _():
        for slot in range(3):
            stats[slot] = local_stats(keep[slot], keep[3 + slot])


def first_logits(pos, got, w, blocks):
    vocab, width = w.shape
    rows = 256
    grid_spec = pltpu.PrefetchScalarGridSpec(
        num_scalar_prefetch=1,
        grid=(vocab // rows,),
        in_specs=[
            pl.BlockSpec(got.shape, lambda i, s: (0, 0)),
            pl.BlockSpec((rows, width), lambda i, s: (i, 0)),
        ] + [ANY] * 6,
        out_specs=[
            pl.BlockSpec((3, rows, LANES), lambda i, s: (0, i, 0)),
            pl.BlockSpec((4, rows, LANES), lambda i, s: (0, i, 0)),
            pl.BlockSpec((3, 8, LANES), lambda i, s: (0, 0, 0)),
        ],
        scratch_shapes=[
            pltpu.VMEM((384, width), jnp.bfloat16),
            pltpu.VMEM((6, vocab, LANES), jnp.float32),
            pltpu.VMEM((4, 16, LANES), jnp.float32),
            pltpu.SemaphoreType.DMA((6,)),
        ],
    )
    return pl.pallas_call(
        first_kernel,
        grid_spec=grid_spec,
        out_shape=[
            jax.ShapeDtypeStruct((3, vocab, LANES), jnp.float32),
            jax.ShapeDtypeStruct((4, vocab, LANES), jnp.float32),
            jax.ShapeDtypeStruct((3, 8, LANES), jnp.float32),
        ],
        compiler_params=params(),
        cost_estimate=cost(2 * vocab * width * 384, vocab * width * 2 + 384 * width * 2),
    )(pos, got, w, *blocks)


def last_kernel(pos, w, target, early, far_a, far_b, far_a2, far_b2, out, send, held, keep, table, sems):
    step = pl.program_id(0)
    z, core = pos[0], pos[1]
    mine, other = core * 64, (1 - core) * 64

    @pl.when(step == 0)
    def _():
        copies = load_blocks(
            [(far_a, mine), (far_b, mine + 32), (far_a2, other), (far_b2, other + 32)], held, sems
        )
        for copy in copies:
            copy.wait()

    rows = w.shape[0]
    logits = dot_nt(w[...], held[...])
    out[...] = logits
    base = pl.multiple_of(step * rows, rows)
    keep[0, pl.ds(base, rows)] = logits
    keep[1, pl.ds(base, rows)] = target[0]

    @pl.when(step == pl.num_programs(0) - 1)
    def _():
        for slot in range(3):
            table[(z + OFFSETS[slot]) % 4] = early[slot]
        table[(z + OFFSETS[3]) % 4] = local_stats(keep[0], keep[1])
        lane = lax.broadcasted_iota(jnp.int32, (32, LANES), 1)
        row = lax.broadcasted_iota(jnp.int32, (32, LANES), 0)
        for block in range(4):
            info = table[block]
            send[:, block * LANES : (block + 1) * LANES] = jnp.broadcast_to(info[0:1], (LANES, LANES))
            extra = jnp.zeros((32, LANES), jnp.float32)
            for kind in range(3):
                for token in range(4):
                    value = jnp.sum(
                        jnp.where(lane == row * 4 + token, info[kind : kind + 1], 0.0), axis=1, keepdims=True
                    )
                    extra = extra + jnp.where(lane == kind * 4 + token, value, 0.0)
            send[block * 32 : (block + 1) * 32, 4 * LANES : 5 * LANES] = extra


def last_logits(pos, w, target, early, blocks):
    vocab, width = w.shape
    rows = 256
    grid_spec = pltpu.PrefetchScalarGridSpec(
        num_scalar_prefetch=1,
        grid=(vocab // rows,),
        in_specs=[
            pl.BlockSpec((rows, width), lambda i, s: (i, 0)),
            pl.BlockSpec((1, rows, LANES), lambda i, s: (3, i, 0)),
            pl.BlockSpec((3, 8, LANES), lambda i, s: (0, 0, 0)),
        ] + [ANY] * 4,
        out_specs=[
            pl.BlockSpec((rows, LANES), lambda i, s: (i, 0)),
            pl.BlockSpec((LANES, 5 * LANES), lambda i, s: (0, 0)),
        ],
        scratch_shapes=[
            pltpu.VMEM((LANES, width), jnp.bfloat16),
            pltpu.VMEM((2, vocab, LANES), jnp.float32),
            pltpu.VMEM((4, 8, LANES), jnp.float32),
            pltpu.SemaphoreType.DMA((4,)),
        ],
    )
    return pl.pallas_call(
        last_kernel,
        grid_spec=grid_spec,
        out_shape=[
            jax.ShapeDtypeStruct((vocab, LANES), jnp.float32),
            jax.ShapeDtypeStruct((LANES, 5 * LANES), jnp.float32),
        ],
        compiler_params=params(),
        cost_estimate=cost(2 * vocab * width * 128, vocab * width * 2),
    )(pos, w, target, early, *blocks)


def grad_of(logits, lse, target):
    return loss_scale * (jnp.exp(logits - lse) - target)


def far_grad_kernel(pos, stats, logits, target, w, mine_out, other_out, grad_out, lse_out, loss_out, left, acc, lse_z):
    step = pl.program_id(0)
    z, core = pos[0], pos[1]

    @pl.when(step == 0)
    def _():
        parts = stats[:, : 4 * LANES]
        peak = jnp.max(parts, axis=0, keepdims=True)
        lse = peak + jnp.log(jnp.sum(jnp.exp(parts - peak), axis=0, keepdims=True))
        for block in range(4):
            lse_z[block] = jnp.broadcast_to(lse[:, block * LANES : (block + 1) * LANES], (8, LANES))
        lse_out[...] = lse_z[...]
        few = stats[:, 4 * LANES :]
        peak = jnp.max(few, axis=0, keepdims=True)
        weight = jnp.exp(few - peak)
        total = jnp.sum(weight, axis=0, keepdims=True)
        mean = jnp.sum(weight * pltpu.roll(few, LANES - 4, 1), axis=0, keepdims=True) / total
        cross = jnp.sum(pltpu.roll(few, LANES - 8, 1), axis=0, keepdims=True)
        lse4 = peak + jnp.log(total)
        row = lax.broadcasted_iota(jnp.int32, (8, LANES), 0)
        loss_out[...] = jnp.where(row == 0, lse4 - cross, lse4 - mean)
        far = lse_z[(z + OFFSETS[3]) % 4]
        grad = grad_of(logits[...], far[0:1], target[0])
        grad_out[...] = grad.astype(jnp.bfloat16)
        left[...] = grad.T.astype(jnp.bfloat16)

    acc[...] = jnp.dot(left[...], w[...], preferred_element_type=jnp.float32)
    mine_out[...] = acc[pl.ds(pl.multiple_of(core * 64, 64), 64)]
    other_out[...] = acc[pl.ds(pl.multiple_of((1 - core) * 64, 64), 64)].astype(jnp.bfloat16)


def far_grad(pos, stats, logits, target, w):
    vocab, width = w.shape
    cols = 768
    grid_spec = pltpu.PrefetchScalarGridSpec(
        num_scalar_prefetch=1,
        grid=(width // cols,),
        in_specs=[
            pl.BlockSpec((LANES, 5 * LANES), lambda i, s: (0, 0)),
            pl.BlockSpec((vocab, LANES), lambda i, s: (0, 0)),
            pl.BlockSpec((1, vocab, LANES), lambda i, s: (3, 0, 0)),
            pl.BlockSpec((vocab, cols), lambda i, s: (0, i)),
        ],
        out_specs=[
            pl.BlockSpec((64, cols), lambda i, s: (0, i)),
            pl.BlockSpec((64, cols), lambda i, s: (0, i)),
            pl.BlockSpec((vocab, LANES), lambda i, s: (0, 0)),
            pl.BlockSpec((4, 8, LANES), lambda i, s: (0, 0, 0)),
            pl.BlockSpec((8, LANES), lambda i, s: (0, 0)),
        ],
        scratch_shapes=[
            pltpu.VMEM((LANES, vocab), jnp.bfloat16),
            pltpu.VMEM((LANES, cols), jnp.float32),
            pltpu.VMEM((4, 8, LANES), jnp.float32),
        ],
    )
    return pl.pallas_call(
        far_grad_kernel,
        grid_spec=grid_spec,
        out_shape=[
            jax.ShapeDtypeStruct((64, width), jnp.float32),
            jax.ShapeDtypeStruct((64, width), jnp.bfloat16),
            jax.ShapeDtypeStruct((vocab, LANES), jnp.bfloat16),
            jax.ShapeDtypeStruct((4, 8, LANES), jnp.float32),
            jax.ShapeDtypeStruct((8, LANES), jnp.float32),
        ],
        compiler_params=params(),
        cost_estimate=cost(2 * vocab * width * 128, vocab * width * 2),
    )(pos, stats, logits, target, w)


def grads_kernel(pos, logits, target, lse, far, wide_out, left_out):
    z = pos[0]
    for slot in range(3):
        row = lse[(z + OFFSETS[slot]) % 4]
        grad = grad_of(logits[slot], row[0:1], target[slot])
        wide_out[:, slot * LANES : (slot + 1) * LANES] = grad.astype(jnp.bfloat16)
        left_out[slot * LANES : (slot + 1) * LANES, :] = grad.T.astype(jnp.bfloat16)
    wide_out[:, 3 * LANES :] = far[...]


def near_grads(pos, logits, target, lse, far):
    vocab = far.shape[0]
    whole = pl.BlockSpec(memory_space=pltpu.VMEM)
    return pl.pallas_call(
        grads_kernel,
        in_specs=[pl.BlockSpec(memory_space=pltpu.SMEM)] + [whole] * 4,
        out_specs=[whole] * 2,
        out_shape=[
            jax.ShapeDtypeStruct((vocab, 4 * LANES), jnp.bfloat16),
            jax.ShapeDtypeStruct((3 * LANES, vocab), jnp.bfloat16),
        ],
        compiler_params=params(),
        cost_estimate=cost(2e6, 5e6),
    )(pos, logits, target, lse, far)


def near_kernel(pos, left, w, mine_out, other_out, own_out, acc):
    core = pos[1]
    acc[...] = jnp.dot(left[...], w[...], preferred_element_type=jnp.float32)
    for slot in range(3):
        mine_out[slot] = acc[pl.ds(pl.multiple_of(slot * 128 + core * 64, 64), 64)]
        part = acc[pl.ds(pl.multiple_of(slot * 128 + (1 - core) * 64, 64), 64)].astype(jnp.bfloat16)
        if slot == 0:
            own_out[...] = part
        else:
            other_out[slot - 1] = part


def near_grad(pos, left, w):
    vocab, width = w.shape
    cols = 768
    grid_spec = pltpu.PrefetchScalarGridSpec(
        num_scalar_prefetch=1,
        grid=(width // cols,),
        in_specs=[
            pl.BlockSpec((3 * LANES, vocab), lambda i, s: (0, 0)),
            pl.BlockSpec((vocab, cols), lambda i, s: (0, i)),
        ],
        out_specs=[
            pl.BlockSpec((3, 64, cols), lambda i, s: (0, 0, i)),
            pl.BlockSpec((2, 64, cols), lambda i, s: (0, 0, i)),
            pl.BlockSpec((64, cols), lambda i, s: (0, i)),
        ],
        scratch_shapes=[pltpu.VMEM((3 * LANES, cols), jnp.float32)],
    )
    return pl.pallas_call(
        near_kernel,
        grid_spec=grid_spec,
        out_shape=[
            jax.ShapeDtypeStruct((3, 64, width), jnp.float32),
            jax.ShapeDtypeStruct((2, 64, width), jnp.bfloat16),
            jax.ShapeDtypeStruct((64, width), jnp.bfloat16),
        ],
        compiler_params=params(),
        cost_estimate=cost(2 * vocab * width * 384, vocab * width * 2),
    )(pos, left, w)


def weight_kernel(pos, grad, own, own2, left, left2, right, right2, far_a, far_b, far_a2, far_b2, out, held, sems):
    core = pos[1]
    mine, other = core * 64, (1 - core) * 64

    @pl.when(pl.program_id(0) == 0)
    def _():
        copies = load_blocks(
            [
                (own, mine), (own2, other), (left, 128 + mine), (left2, 128 + other),
                (right, 256 + mine), (right2, 256 + other),
                (far_a, 384 + mine), (far_b, 384 + mine + 32), (far_a2, 384 + other), (far_b2, 384 + other + 32),
            ],
            held, sems,
        )
        for copy in copies:
            copy.wait()

    width = out.shape[1]
    cols = 768
    for tile in range(width // cols):
        at = slice(tile * cols, (tile + 1) * cols)
        out[:, at] = jnp.dot(grad[...], held[:, at], preferred_element_type=jnp.float32).astype(jnp.bfloat16)


def weight_grad(pos, grad, blocks, width):
    vocab, tokens = grad.shape
    rows = 256
    grid_spec = pltpu.PrefetchScalarGridSpec(
        num_scalar_prefetch=1,
        grid=(vocab // rows,),
        in_specs=[pl.BlockSpec((rows, tokens), lambda i, s: (i, 0))] + [ANY] * 10,
        out_specs=pl.BlockSpec((rows, width), lambda i, s: (i, 0)),
        scratch_shapes=[pltpu.VMEM((tokens, width), jnp.bfloat16), pltpu.SemaphoreType.DMA((10,))],
    )
    return pl.pallas_call(
        weight_kernel,
        grid_spec=grid_spec,
        out_shape=jax.ShapeDtypeStruct((vocab, width), jnp.bfloat16),
        compiler_params=params(),
        cost_estimate=cost(2 * vocab * width * tokens, vocab * width * 2 + tokens * width * 2),
    )(pos, grad, *blocks)


def body(hidden, head_weight, teacher_logits, teacher_ids):
    seq_count = lax.axis_size("seq")
    vocab_count = lax.axis_size("vocab")
    owners = seq_count * vocab_count
    vocab_rows, width = head_weight.shape
    tok_rows, feat_part = hidden.shape
    seq_index = lax.axis_index("seq")
    pos = jnp.stack([seq_index // 2, seq_index % 2]).astype(jnp.int32)
    up = [(i, (i + 2) % seq_count) for i in range(seq_count)]
    down = [(i, (i - 2) % seq_count) for i in range(seq_count)]
    twin = [(i, i ^ 1) for i in range(seq_count)]

    def move(x, perm):
        return lax.ppermute(x, "seq", perm)

    f32 = jnp.float32
    bf16 = jnp.bfloat16
    half = tok_rows // 2

    spread = jnp.broadcast_to(hidden[None], (vocab_count, tok_rows, feat_part))
    spread = lax.all_to_all(spread, "vocab", split_axis=0, concat_axis=0, tiled=True)
    own = spread.transpose(1, 0, 2).reshape(tok_rows, width)
    left = move(own, up)
    right = move(own, down)
    own2 = move(own, twin)
    teach = teacher_rows(owners, vocab_rows, teacher_logits, teacher_ids)
    teach, _ = lax.optimization_barrier((teach, own))
    got = lax.all_to_all(teach, BOTH, split_axis=0, concat_axis=0, tiled=True)
    far_a = move(left[:half], up)
    far_b = move(right[half:], down)
    left2 = move(left, twin)
    right2 = move(right, twin)
    near_blocks = (own, own2, left, left2, right, right2)
    logits, target, early = first_logits(pos, got, head_weight, near_blocks)
    far_blocks = (far_a, far_b, move(far_a, twin), move(far_b, twin))
    far_logits, send = last_logits(pos, head_weight, target, early, far_blocks)
    stats = lax.all_to_all(send, BOTH, split_axis=0, concat_axis=0, tiled=True)

    far_mine, far_other, grad_far, lse, loss = far_grad(pos, stats, far_logits, target, head_weight)
    far_swap = move(far_other, twin)
    wide, left_grad = near_grads(pos, logits, target, lse, grad_far)
    far_sum = (far_mine + far_swap.astype(f32)).astype(bf16)
    go_up = move(far_sum[:half], up)
    go_down = move(far_sum[half:], down)
    mine, other, own_other = near_grad(pos, left_grad, head_weight)
    swap = move(other, twin)
    own_swap = move(own_other, twin)
    to_left = mine[1] + swap[0].astype(f32)
    to_right = mine[2] + swap[1].astype(f32)
    right_b = move(to_right[half:].astype(bf16), up)
    left_b = move(to_left[:half].astype(bf16), down)
    right_a = move((to_right[:half] + go_up.astype(f32)).astype(bf16), up)
    left_a = move((to_left[half:] + go_down.astype(f32)).astype(bf16), down)
    grad_weight = weight_grad(pos, wide, near_blocks + far_blocks, width)
    own_sum = mine[0] + own_swap.astype(f32)
    upper = own_sum[:half] + right_a.astype(f32) + left_b.astype(f32)
    lower = own_sum[half:] + right_b.astype(f32) + left_a.astype(f32)
    total = jnp.concatenate([upper, lower], axis=0).astype(bf16)
    parts = total.reshape(tok_rows, vocab_count, feat_part).transpose(1, 0, 2)
    parts = lax.all_to_all(parts, "vocab", split_axis=0, concat_axis=0, tiled=True)
    grad_hidden = jnp.sum(parts.astype(f32), axis=0).astype(bf16)
    rows = teacher_logits.shape[0]
    return loss[0, :rows], loss[1, :rows], grad_hidden, grad_weight


def solution(mesh):
    placed = (
        P("seq", "vocab"),
        P(("seq", "vocab"), None),
        P(("seq", "vocab"), None),
        P(("seq", "vocab"), None),
    )
    return jax.shard_map(
        body,
        mesh=mesh,
        in_specs=placed,
        out_specs=(
            P(("seq", "vocab")),
            P(("seq", "vocab")),
            P("seq", "vocab"),
            P(("seq", "vocab"), None),
        ),
        check_vma=False,
    )
```

```python
import functools

import jax
import jax.numpy as jnp
from jax import lax
from jax.experimental import pallas as pl
from jax.experimental.pallas import tpu as pltpu
from jax.sharding import PartitionSpec as P

loss_scale = 64.0
SLOTS = 6
OFFSETS = (0, 3, 1, 2)
LANES = 128
COLS = 768
ANY = pl.BlockSpec(memory_space=pl.ANY)
WHOLE = pl.BlockSpec(memory_space=pltpu.VMEM)
FAR = pl.BlockSpec(memory_space=pltpu.HBM)
SCALARS = pl.BlockSpec(memory_space=pltpu.SMEM)
VMEM_LIMIT = 16 * 1024 * 1024
BOTH = ("seq", "vocab")


def params():
    return pltpu.CompilerParams(vmem_limit_bytes=VMEM_LIMIT)


def cost(flops, nbytes):
    return pl.CostEstimate(flops=int(flops), bytes_accessed=int(nbytes), transcendentals=0)


def teacher_kernel(owners, vocab_rows, logits_ref, ids_ref, out_ref):
    rows, width = logits_ref.shape
    scores = logits_ref[...]
    expo = jnp.exp(scores - jnp.max(scores, axis=1, keepdims=True))
    prob = expo / jnp.sum(expo, axis=1, keepdims=True)
    ids = ids_ref[...]
    shift = vocab_rows.bit_length() - 1
    owner_iota = lax.broadcasted_iota(jnp.int32, (owners, width), 0)
    slot_iota = lax.broadcasted_iota(jnp.int32, (owners, width), 1)
    lane = lax.broadcasted_iota(jnp.int32, (owners, rows * 16), 1)
    out = jnp.zeros((owners, rows * 16), jnp.float32)
    for row in range(rows):
        row_ids = jnp.broadcast_to(ids[row : row + 1, :], (owners, width))
        row_prob = jnp.broadcast_to(prob[row : row + 1, :], (owners, width))
        owner = lax.shift_right_logical(row_ids, shift)
        start = jnp.sum((owner < owner_iota).astype(jnp.int32), axis=1, keepdims=True)
        place = jnp.where(owner == owner_iota, slot_iota - start, -1)
        local = (row_ids - owner * vocab_rows + 1).astype(jnp.float32)
        for slot in range(SLOTS):
            hit = place == slot
            value = jnp.sum(jnp.where(hit, row_prob, 0.0), axis=1, keepdims=True)
            index = jnp.sum(jnp.where(hit, local, 0.0), axis=1, keepdims=True) - 1.0
            out = out + jnp.where(lane == row * 16 + slot, value, 0.0)
            out = out + jnp.where(lane == row * 16 + 8 + slot, index, 0.0)
    out_ref[...] = out


def teacher_rows(owners, vocab_rows, teacher_logits, teacher_ids):
    rows = teacher_logits.shape[0]
    return pl.pallas_call(
        functools.partial(teacher_kernel, owners, vocab_rows),
        out_shape=jax.ShapeDtypeStruct((owners, rows * 16), jnp.float32),
        compiler_params=params(),
        cost_estimate=cost(4e6, 40000),
    )(teacher_logits, teacher_ids)


def dot_nt(a, b):
    return lax.dot_general(a, b, (((1,), (1,)), ((), ())), preferred_element_type=jnp.float32)


def local_stats(logits, target):
    peak = jnp.max(logits, axis=0, keepdims=True)
    expo = jnp.exp(logits - peak)
    total = jnp.sum(expo, axis=0, keepdims=True)
    mean = jnp.sum(expo * logits, axis=0, keepdims=True) / total
    cross = jnp.sum(target * logits, axis=0, keepdims=True)
    lse = peak + jnp.log(total)
    row = lax.broadcasted_iota(jnp.int32, (8, LANES), 0)
    return jnp.where(row == 0, lse, jnp.where(row == 1, mean, jnp.where(row == 2, cross, 0.0)))


def load_blocks(pieces, dest, sems):
    copies = [
        pltpu.make_async_copy(src, dest.at[pl.ds(pl.multiple_of(row, 32), src.shape[0])], sems.at[k])
        for k, (src, row) in enumerate(pieces)
    ]
    for copy in copies:
        copy.start()
    return copies


def first_kernel(pos, got, source, own, own2, left, left2, right, right2, w, out, target, stats, held, teach, sems):
    z, core = pos[0], pos[1]
    count = sems.shape[0]
    chunk = source.shape[0] // count
    copies = [
        pltpu.make_async_copy(source.at[pl.ds(k * chunk, chunk)], w.at[pl.ds(k * chunk, chunk)], sems.at[k])
        for k in range(count)
    ]
    for copy in copies:
        copy.start()
    for slot, mine, other in ((0, own, own2), (1, left, left2), (2, right, right2)):
        held[pl.ds(pl.multiple_of(slot * 128 + core * 64, 64), 64)] = mine[...]
        held[pl.ds(pl.multiple_of(slot * 128 + (1 - core) * 64, 64), 64)] = other[...]
    flipped = got[...].T
    source_row = lax.broadcasted_iota(jnp.int32, (LANES, 4 * LANES), 0)
    token = lax.broadcasted_iota(jnp.int32, (LANES, 4 * LANES), 1)
    spread = jnp.zeros((16, 4 * LANES), jnp.float32)
    for row in range(4):
        pick = (token == source_row * 4 + row).astype(jnp.float32)
        spread = spread + jnp.dot(
            flipped[row * 16 : row * 16 + 16], pick,
            precision=lax.Precision.HIGHEST, preferred_element_type=jnp.float32,
        )
    for block in range(4):
        teach[block] = spread[:, block * LANES : (block + 1) * LANES]
    rows = 64

    @pl.loop(0, w.shape[0] // rows)
    def _(step):
        base = pl.multiple_of(step * rows, rows)
        word = (lax.broadcasted_iota(jnp.int32, (rows, LANES), 0) + step * rows).astype(jnp.float32)
        for slot in range(4):
            info = teach[(z + OFFSETS[slot]) % 4]
            dense = jnp.zeros((rows, LANES), jnp.float32)
            for k in range(SLOTS):
                dense = dense + jnp.where(word == info[8 + k : 9 + k], info[k : k + 1], 0.0)
            target[slot, pl.ds(base, rows)] = dense

    for k in range(count):
        copies[k].wait()
        at = slice(k * chunk, (k + 1) * chunk)
        logits = dot_nt(w[at], held[...])
        for slot in range(3):
            out[slot, at] = logits[:, slot * LANES : (slot + 1) * LANES]
    for slot in range(3):
        stats[slot] = local_stats(out[slot], target[slot])


def first_logits(pos, got, source, blocks):
    vocab, width = source.shape
    return pl.pallas_call(
        first_kernel,
        in_specs=[SCALARS, WHOLE, FAR] + [WHOLE] * 6,
        out_specs=[WHOLE] * 5,
        out_shape=[
            pltpu.VMEM((vocab, width), jnp.bfloat16),
            jax.ShapeDtypeStruct((3, vocab, LANES), jnp.float32),
            jax.ShapeDtypeStruct((4, vocab, LANES), jnp.float32),
            jax.ShapeDtypeStruct((3, 8, LANES), jnp.float32),
            jax.ShapeDtypeStruct((3 * LANES, width), jnp.bfloat16),
        ],
        scratch_shapes=[pltpu.VMEM((4, 16, LANES), jnp.float32), pltpu.SemaphoreType.DMA((2,))],
        compiler_params=params(),
        cost_estimate=cost(1000, 1000),
    )(pos, got, pltpu.with_memory_space_constraint(source, pltpu.HBM), *blocks)


def last_kernel(pos, w, target, early, far_a, far_b, far_a2, far_b2, out, send, held, table, sems):
    z, core = pos[0], pos[1]
    mine, other = core * 64, (1 - core) * 64
    copies = load_blocks(
        [(far_a, mine), (far_b, mine + 32), (far_a2, other), (far_b2, other + 32)], held, sems
    )
    for copy in copies:
        copy.wait()
    out[...] = dot_nt(w[...], held[...])
    for slot in range(3):
        table[(z + OFFSETS[slot]) % 4] = early[slot]
    table[(z + OFFSETS[3]) % 4] = local_stats(out[...], target[3])
    lane = lax.broadcasted_iota(jnp.int32, (32, LANES), 1)
    row = lax.broadcasted_iota(jnp.int32, (32, LANES), 0)
    for block in range(4):
        info = table[block]
        send[:, block * LANES : (block + 1) * LANES] = jnp.broadcast_to(info[0:1], (LANES, LANES))
        extra = jnp.zeros((32, LANES), jnp.float32)
        for kind in range(3):
            for token in range(4):
                value = jnp.sum(
                    jnp.where(lane == row * 4 + token, info[kind : kind + 1], 0.0), axis=1, keepdims=True
                )
                extra = extra + jnp.where(lane == kind * 4 + token, value, 0.0)
        send[block * 32 : (block + 1) * 32, 4 * LANES : 5 * LANES] = extra


def last_logits(pos, w, target, early, blocks):
    vocab, width = w.shape
    return pl.pallas_call(
        last_kernel,
        in_specs=[SCALARS] + [WHOLE] * 3 + [ANY] * 4,
        out_specs=[WHOLE] * 3,
        out_shape=[
            jax.ShapeDtypeStruct((vocab, LANES), jnp.float32),
            jax.ShapeDtypeStruct((LANES, 5 * LANES), jnp.float32),
            jax.ShapeDtypeStruct((LANES, width), jnp.bfloat16),
        ],
        scratch_shapes=[pltpu.VMEM((4, 8, LANES), jnp.float32), pltpu.SemaphoreType.DMA((4,))],
        compiler_params=params(),
        cost_estimate=cost(2 * vocab * width * 128, vocab * width * 2),
    )(pos, w, target, early, *blocks)


def grad_of(logits, lse, target):
    return loss_scale * (jnp.exp(logits - lse) - target)


def split_rows(pos, acc, at, base, mine_out, other_out):
    core = pos[1]
    mine_out[:, at] = acc[pl.ds(pl.multiple_of(base + core * 64, 64), 64)]
    other_out[:, at] = acc[pl.ds(pl.multiple_of(base + (1 - core) * 64, 64), 64)].astype(jnp.bfloat16)


def far_grad_kernel(pos, stats, logits, target, w, mine_out, other_out, grad_out, lse_out, loss_out, acc):
    z = pos[0]
    parts = stats[:, : 4 * LANES]
    peak = jnp.max(parts, axis=0, keepdims=True)
    lse = peak + jnp.log(jnp.sum(jnp.exp(parts - peak), axis=0, keepdims=True))
    for block in range(4):
        lse_out[block] = jnp.broadcast_to(lse[:, block * LANES : (block + 1) * LANES], (8, LANES))
    few = stats[:, 4 * LANES :]
    peak = jnp.max(few, axis=0, keepdims=True)
    weight = jnp.exp(few - peak)
    total = jnp.sum(weight, axis=0, keepdims=True)
    mean = jnp.sum(weight * pltpu.roll(few, LANES - 4, 1), axis=0, keepdims=True) / total
    cross = jnp.sum(pltpu.roll(few, LANES - 8, 1), axis=0, keepdims=True)
    lse4 = peak + jnp.log(total)
    row = lax.broadcasted_iota(jnp.int32, (8, LANES), 0)
    loss_out[...] = jnp.where(row == 0, lse4 - cross, lse4 - mean)
    far = lse_out[(z + OFFSETS[3]) % 4]
    grad = grad_of(logits[...], far[0:1], target[3])
    grad_out[...] = grad.astype(jnp.bfloat16)
    left = grad.T.astype(jnp.bfloat16)
    for tile in range(w.shape[1] // COLS):
        at = slice(tile * COLS, (tile + 1) * COLS)
        acc[...] = jnp.dot(left, w[:, at], preferred_element_type=jnp.float32)
        split_rows(pos, acc, at, 0, mine_out, other_out)


def far_grad(pos, stats, logits, target, w):
    vocab, width = w.shape
    return pl.pallas_call(
        far_grad_kernel,
        in_specs=[SCALARS] + [WHOLE] * 4,
        out_specs=[WHOLE] * 5,
        out_shape=[
            jax.ShapeDtypeStruct((64, width), jnp.float32),
            jax.ShapeDtypeStruct((64, width), jnp.bfloat16),
            jax.ShapeDtypeStruct((vocab, LANES), jnp.bfloat16),
            jax.ShapeDtypeStruct((4, 8, LANES), jnp.float32),
            jax.ShapeDtypeStruct((8, LANES), jnp.float32),
        ],
        scratch_shapes=[pltpu.VMEM((LANES, COLS), jnp.float32)],
        compiler_params=params(),
        cost_estimate=cost(2 * vocab * width * 128, vocab * width * 2),
    )(pos, stats, logits, target, w)


def grads_kernel(pos, logits, target, lse, far, wide_out, left_out):
    z = pos[0]
    for slot in range(3):
        row = lse[(z + OFFSETS[slot]) % 4]
        grad = grad_of(logits[slot], row[0:1], target[slot])
        wide_out[:, slot * LANES : (slot + 1) * LANES] = grad.astype(jnp.bfloat16)
        left_out[slot * LANES : (slot + 1) * LANES, :] = grad.T.astype(jnp.bfloat16)
    wide_out[:, 3 * LANES :] = far[...]


def near_grads(pos, logits, target, lse, far):
    vocab = far.shape[0]
    return pl.pallas_call(
        grads_kernel,
        in_specs=[SCALARS] + [WHOLE] * 4,
        out_specs=[WHOLE] * 2,
        out_shape=[
            jax.ShapeDtypeStruct((vocab, 4 * LANES), jnp.bfloat16),
            jax.ShapeDtypeStruct((3 * LANES, vocab), jnp.bfloat16),
        ],
        compiler_params=params(),
        cost_estimate=cost(2e6, 5e6),
    )(pos, logits, target, lse, far)


def near_kernel(pos, left, w, mine_out, other_out, acc):
    core = pos[1]
    for tile in range(w.shape[1] // COLS):
        at = slice(tile * COLS, (tile + 1) * COLS)
        acc[...] = jnp.dot(left[...], w[:, at], preferred_element_type=jnp.float32)
        for slot in range(3):
            to = slice(slot * 64, (slot + 1) * 64)
            mine_out[to, at] = acc[pl.ds(pl.multiple_of(slot * 128 + core * 64, 64), 64)]
            part = acc[pl.ds(pl.multiple_of(slot * 128 + (1 - core) * 64, 64), 64)]
            other_out[to, at] = part.astype(jnp.bfloat16)


def near_grad(pos, left, w):
    vocab, width = w.shape
    tokens = left.shape[0]
    return pl.pallas_call(
        near_kernel,
        in_specs=[SCALARS] + [WHOLE] * 2,
        out_specs=[WHOLE] * 2,
        out_shape=[
            jax.ShapeDtypeStruct((tokens // 2, width), jnp.float32),
            jax.ShapeDtypeStruct((tokens // 2, width), jnp.bfloat16),
        ],
        scratch_shapes=[pltpu.VMEM((tokens, COLS), jnp.float32)],
        compiler_params=params(),
        cost_estimate=cost(2 * vocab * width * tokens, vocab * width * 2),
    )(pos, left, w)


def weight_kernel(grad, near, far, out):
    for tile in range(out.shape[1] // COLS):
        at = slice(tile * COLS, (tile + 1) * COLS)
        held = jnp.concatenate([near[:, at], far[:, at]], axis=0)
        out[:, at] = jnp.dot(grad[...], held, preferred_element_type=jnp.float32).astype(jnp.bfloat16)


def weight_grad(grad, near, far):
    vocab, tokens = grad.shape
    width = near.shape[1]
    rows = 256
    return pl.pallas_call(
        weight_kernel,
        grid=(vocab // rows,),
        in_specs=[pl.BlockSpec((rows, tokens), lambda i: (i, 0)), WHOLE, WHOLE],
        out_specs=pl.BlockSpec((rows, width), lambda i: (i, 0)),
        out_shape=jax.ShapeDtypeStruct((vocab, width), jnp.bfloat16),
        compiler_params=params(),
        cost_estimate=cost(2 * vocab * width * tokens, vocab * width * 2 + tokens * width * 2),
    )(grad, near, far)


def widen_kernel(upper, lower, out):
    out[0] = upper[...].astype(jnp.float32)
    out[1] = lower[...].astype(jnp.float32)


def widen(upper, lower):
    return pl.pallas_call(
        widen_kernel,
        in_specs=[WHOLE] * 2,
        out_specs=WHOLE,
        out_shape=jax.ShapeDtypeStruct((2, *upper.shape), jnp.float32),
        compiler_params=params(),
        cost_estimate=cost(1e11, 1e9),
    )(upper, lower)


def fold_kernel(near, from_left, from_right, out, total):
    rows = from_left.shape[0]
    total[...] = near[:rows] + from_left[...].astype(jnp.float32) + from_right[...].astype(jnp.float32)
    part = out.shape[2]
    for index in range(out.shape[0]):
        out[index] = total[:, index * part : (index + 1) * part].astype(jnp.bfloat16)


def fold(count, pieces):
    rows, width = pieces[1].shape
    return pl.pallas_call(
        fold_kernel,
        in_specs=[WHOLE] * 3,
        out_specs=WHOLE,
        out_shape=jax.ShapeDtypeStruct((count, rows, width // count), jnp.bfloat16),
        scratch_shapes=[pltpu.VMEM((rows, width), jnp.float32)],
        compiler_params=params(),
        cost_estimate=cost(2e6, 4e6),
    )(*pieces)


def sum_kernel(parts, out):
    total = parts[0].astype(jnp.float32)
    for index in range(1, parts.shape[0]):
        total = total + parts[index].astype(jnp.float32)
    out[...] = total.astype(jnp.bfloat16)


def sum_parts(parts):
    return pl.pallas_call(
        sum_kernel,
        in_specs=[WHOLE],
        out_specs=WHOLE,
        out_shape=jax.ShapeDtypeStruct(parts.shape[1:], jnp.bfloat16),
        compiler_params=params(),
        cost_estimate=cost(4e5, 8e5),
    )(parts)


def body(hidden, head_weight, teacher_logits, teacher_ids):
    seq_count = lax.axis_size("seq")
    vocab_count = lax.axis_size("vocab")
    owners = seq_count * vocab_count
    vocab_rows, width = head_weight.shape
    tok_rows, feat_part = hidden.shape
    seq_index = lax.axis_index("seq")
    pos = jnp.stack([seq_index // 2, seq_index % 2]).astype(jnp.int32)
    up = [(i, (i + 2) % seq_count) for i in range(seq_count)]
    down = [(i, (i - 2) % seq_count) for i in range(seq_count)]
    twin = [(i, i ^ 1) for i in range(seq_count)]

    def move(x, perm):
        return lax.ppermute(x, "seq", perm)

    def after(x, *before):
        return lax.optimization_barrier((x, before))[0]

    f32 = jnp.float32
    bf16 = jnp.bfloat16
    half = tok_rows // 2

    spread = jnp.broadcast_to(hidden[None], (vocab_count, tok_rows, feat_part))
    spread = lax.all_to_all(spread, "vocab", split_axis=0, concat_axis=0, tiled=True)
    teach = teacher_rows(owners, vocab_rows, teacher_logits, teacher_ids)
    spread, (teach, pos) = lax.optimization_barrier((spread, (teach, pos)))
    own = spread.transpose(1, 0, 2).reshape(tok_rows, width)
    left = move(own, up)
    right = move(own, down)
    own2 = move(own, twin)
    teach = after(teach, own)
    got = lax.all_to_all(teach, BOTH, split_axis=0, concat_axis=0, tiled=True)
    left, right = after((left, right), got)
    far_a = move(left[:half], up)
    far_b = move(right[half:], down)
    near_blocks = (own, own2, left, move(left, twin), right, move(right, twin))
    weight, logits, target, early, near_rows = first_logits(pos, got, head_weight, near_blocks)
    far_a, far_b = after((far_a, far_b), early)
    far_blocks = (far_a, far_b, move(far_a, twin), move(far_b, twin))
    far_logits, send, far_rows = last_logits(pos, weight, target, early, far_blocks)
    stats = lax.all_to_all(send, BOTH, split_axis=0, concat_axis=0, tiled=True)

    far_mine, far_other, grad_far, lse, loss = far_grad(pos, stats, far_logits, target, weight)
    far_swap = move(far_other, twin)
    wide, near_left = near_grads(pos, logits, target, lse, grad_far)
    far_sum = (far_mine + far_swap.astype(f32)).astype(bf16)
    go_up = move(far_sum[:half], up)
    go_down = move(far_sum[half:], down)
    near_left = after(near_left, far_sum)
    mine, other = near_grad(pos, near_left, weight)
    swap = move(other, twin)
    passed = widen(go_up, go_down)
    swap = after(swap, passed)
    near_sum = mine + swap.astype(f32)
    to_right = near_sum[2 * tok_rows :]
    to_right = jnp.concatenate([to_right[:half] + passed[0], to_right[half:]]).astype(bf16)
    to_left = near_sum[tok_rows : 2 * tok_rows]
    to_left = jnp.concatenate([to_left[:half], to_left[half:] + passed[1]]).astype(bf16)
    from_left = move(to_right, up)
    from_right = move(to_left, down)
    grad_weight = weight_grad(wide, near_rows, far_rows)
    parts = fold(vocab_count, (near_sum, from_left, from_right))
    parts = lax.all_to_all(parts, "vocab", split_axis=0, concat_axis=0, tiled=True)
    grad_hidden = sum_parts(parts)
    rows = teacher_logits.shape[0]
    return loss[0, :rows], loss[1, :rows], grad_hidden, grad_weight


def solution(mesh):
    placed = (
        P("seq", "vocab"),
        P(("seq", "vocab"), None),
        P(("seq", "vocab"), None),
        P(("seq", "vocab"), None),
    )
    return jax.shard_map(
        body,
        mesh=mesh,
        in_specs=placed,
        out_specs=(
            P(("seq", "vocab")),
            P(("seq", "vocab")),
            P("seq", "vocab"),
            P(("seq", "vocab"), None),
        ),
        check_vma=False,
    )
```

```python
import functools

import jax
import jax.numpy as jnp
from jax import lax
from jax.experimental import pallas as pl
from jax.experimental.pallas import tpu as pltpu
from jax.sharding import PartitionSpec as P

loss_scale = 64.0
SLOTS = 6
OFFSETS = (0, 3, 1, 2)
LANES = 128
COLS = 768
ANY = pl.BlockSpec(memory_space=pl.ANY)
WHOLE = pl.BlockSpec(memory_space=pltpu.VMEM)
FAR = pl.BlockSpec(memory_space=pltpu.HBM)
SCALARS = pl.BlockSpec(memory_space=pltpu.SMEM)
VMEM_LIMIT = 16 * 1024 * 1024
BOTH = ("seq", "vocab")


def params():
    return pltpu.CompilerParams(vmem_limit_bytes=VMEM_LIMIT)


def cost(flops, nbytes):
    return pl.CostEstimate(flops=int(flops), bytes_accessed=int(nbytes), transcendentals=0)


def teacher_kernel(owners, vocab_rows, logits_ref, ids_ref, out_ref):
    rows, width = logits_ref.shape
    scores = logits_ref[...]
    expo = jnp.exp(scores - jnp.max(scores, axis=1, keepdims=True))
    prob = expo / jnp.sum(expo, axis=1, keepdims=True)
    ids = ids_ref[...]
    shift = vocab_rows.bit_length() - 1
    owner_of = lax.shift_right_logical(ids, shift)
    local_of = (ids - owner_of * vocab_rows + 1).astype(jnp.float32)
    owner_of = owner_of.astype(jnp.float32)
    owner_iota = lax.broadcasted_iota(jnp.int32, (owners, width), 0).astype(jnp.float32)
    slot_iota = lax.broadcasted_iota(jnp.int32, (owners, width), 1).astype(jnp.float32)
    lane = lax.broadcasted_iota(jnp.int32, (owners, rows * 16), 1)
    out = jnp.zeros((owners, rows * 16), jnp.float32)
    for row in range(rows):
        row_prob = jnp.broadcast_to(prob[row : row + 1, :], (owners, width))
        owner = jnp.broadcast_to(owner_of[row : row + 1, :], (owners, width))
        local = jnp.broadcast_to(local_of[row : row + 1, :], (owners, width))
        same = owner == owner_iota
        start = jnp.sum(jnp.where(owner < owner_iota, 1.0, 0.0), axis=1, keepdims=True)
        place = jnp.where(same, slot_iota - start, -1.0)
        for slot in range(2):
            hit = place == slot
            value = jnp.sum(jnp.where(hit, row_prob, 0.0), axis=1, keepdims=True)
            index = jnp.sum(jnp.where(hit, local, 0.0), axis=1, keepdims=True) - 1.0
            out = out + jnp.where(lane == row * 16 + slot, value, jnp.where(lane == row * 16 + 8 + slot, index, 0.0))
        many = jnp.sum(jnp.where(same, 1.0, 0.0), axis=1, keepdims=True) > 2.0
        first = jnp.sum(jnp.where(many, start, 0.0), axis=0, keepdims=True)
        hot_place = slot_iota[:1] - first
        hot_index = local_of[row : row + 1, :]
        extra = jnp.zeros((1, rows * 16), jnp.float32)
        for slot in range(2, SLOTS):
            hit = hot_place == slot
            value = jnp.sum(jnp.where(hit, prob[row : row + 1, :], 0.0), axis=1, keepdims=True)
            index = jnp.sum(jnp.where(hit, hot_index, 0.0), axis=1, keepdims=True)
            at = lane[:1]
            extra = extra + jnp.where(at == row * 16 + slot, value, jnp.where(at == row * 16 + 8 + slot, index, 0.0))
        empty = (lane >= row * 16 + 10) & (lane < row * 16 + 8 + SLOTS)
        out = out + jnp.where(many, extra, 0.0) - empty.astype(jnp.float32)
    out_ref[...] = out


def teacher_rows(owners, vocab_rows, teacher_logits, teacher_ids):
    rows = teacher_logits.shape[0]
    return pl.pallas_call(
        functools.partial(teacher_kernel, owners, vocab_rows),
        out_shape=jax.ShapeDtypeStruct((owners, rows * 16), jnp.float32),
        compiler_params=params(),
        cost_estimate=cost(4e6, 40000),
    )(teacher_logits, teacher_ids)


def copies_kernel(block, out):
    for index in range(out.shape[0]):
        out[index] = block[...]


def copies_of(block, count):
    return pl.pallas_call(
        copies_kernel,
        in_specs=[WHOLE],
        out_specs=WHOLE,
        out_shape=jax.ShapeDtypeStruct((count, *block.shape), block.dtype),
        compiler_params=params(),
        cost_estimate=cost(1000, 1e6),
    )(block)


def join_kernel(parts, out, rows):
    part = parts.shape[2]
    for index in range(parts.shape[0]):
        rows[:, index * part : (index + 1) * part] = parts[index].astype(jnp.float32)
    out[...] = rows[...].astype(jnp.bfloat16)


def join_parts(parts):
    count, rows, part = parts.shape
    return pl.pallas_call(
        join_kernel,
        in_specs=[WHOLE],
        out_specs=WHOLE,
        out_shape=jax.ShapeDtypeStruct((rows, count * part), parts.dtype),
        scratch_shapes=[pltpu.VMEM((rows, count * part), jnp.float32)],
        compiler_params=params(),
        cost_estimate=cost(1e6, 2e6),
    )(parts)


def dot_nt(a, b):
    return lax.dot_general(a, b, (((1,), (1,)), ((), ())), preferred_element_type=jnp.float32)


def local_stats(logits, target):
    peak = jnp.max(logits, axis=0, keepdims=True)
    expo = jnp.exp(logits - peak)
    total = jnp.sum(expo, axis=0, keepdims=True)
    mean = jnp.sum(expo * logits, axis=0, keepdims=True) / total
    cross = jnp.sum(target * logits, axis=0, keepdims=True)
    lse = peak + jnp.log(total)
    row = lax.broadcasted_iota(jnp.int32, (8, LANES), 0)
    return jnp.where(row == 0, lse, jnp.where(row == 1, mean, jnp.where(row == 2, cross, 0.0)))


def first_kernel(pos, got, source, own, own2, left, left2, right, right2, w, out, target, held, teach, sems):
    z, core = pos[0], pos[1]
    count = sems.shape[0]
    chunk = source.shape[0] // count
    copies = [
        pltpu.make_async_copy(source.at[pl.ds(k * chunk, chunk)], w.at[pl.ds(k * chunk, chunk)], sems.at[k])
        for k in range(count)
    ]
    for copy in copies:
        copy.start()
    for slot, mine, other in ((0, own, own2), (1, left, left2), (2, right, right2)):
        held[pl.ds(pl.multiple_of(slot * 128 + core * 64, 64), 64)] = mine[...]
        held[pl.ds(pl.multiple_of(slot * 128 + (1 - core) * 64, 64), 64)] = other[...]
    flipped = got[...].T
    source_row = lax.broadcasted_iota(jnp.int32, (LANES, 4 * LANES), 0)
    token = lax.broadcasted_iota(jnp.int32, (LANES, 4 * LANES), 1)
    spread = jnp.zeros((16, 4 * LANES), jnp.float32)
    for row in range(4):
        pick = (token == source_row * 4 + row).astype(jnp.float32)
        spread = spread + jnp.dot(
            flipped[row * 16 : row * 16 + 16], pick,
            precision=lax.Precision.HIGHEST, preferred_element_type=jnp.float32,
        )
    for block in range(4):
        teach[block] = spread[:, block * LANES : (block + 1) * LANES]
    rows = 64

    @pl.loop(0, w.shape[0] // rows)
    def _(step):
        base = pl.multiple_of(step * rows, rows)
        word = (lax.broadcasted_iota(jnp.int32, (rows, LANES), 0) + step * rows).astype(jnp.float32)
        for slot in range(4):
            info = teach[(z + OFFSETS[slot]) % 4]
            dense = jnp.zeros((rows, LANES), jnp.float32)
            for k in range(SLOTS):
                dense = dense + jnp.where(word == info[8 + k : 9 + k], info[k : k + 1], 0.0)
            target[slot, pl.ds(base, rows)] = dense

    for k in range(count):
        copies[k].wait()
        at = slice(k * chunk, (k + 1) * chunk)
        logits = dot_nt(w[at], held[...])
        for slot in range(3):
            out[slot, at] = logits[:, slot * LANES : (slot + 1) * LANES]


def first_logits(pos, got, source, blocks):
    vocab, width = source.shape
    return pl.pallas_call(
        first_kernel,
        in_specs=[SCALARS, WHOLE, FAR] + [WHOLE] * 6,
        out_specs=[WHOLE] * 4,
        out_shape=[
            pltpu.VMEM((vocab, width), jnp.bfloat16),
            jax.ShapeDtypeStruct((3, vocab, LANES), jnp.float32),
            jax.ShapeDtypeStruct((4, vocab, LANES), jnp.float32),
            jax.ShapeDtypeStruct((3 * LANES, width), jnp.bfloat16),
        ],
        scratch_shapes=[pltpu.VMEM((4, 16, LANES), jnp.float32), pltpu.SemaphoreType.DMA((2,))],
        compiler_params=params(),
        cost_estimate=cost(1000, 1000),
    )(pos, got, pltpu.with_memory_space_constraint(source, pltpu.HBM), *blocks)


def spread_stats(info):
    lane = lax.broadcasted_iota(jnp.int32, (32, LANES), 1)
    row = lax.broadcasted_iota(jnp.int32, (32, LANES), 0)
    extra = jnp.zeros((32, LANES), jnp.float32)
    for kind in range(3):
        for token in range(4):
            value = jnp.sum(jnp.where(lane == row * 4 + token, info[kind : kind + 1], 0.0), axis=1, keepdims=True)
            extra = extra + jnp.where(lane == kind * 4 + token, value, 0.0)
    return extra


def fill_send(send, block, info):
    send[:, pl.ds(pl.multiple_of(block * LANES, LANES), LANES)] = jnp.broadcast_to(info[0:1], (LANES, LANES))
    send[pl.ds(pl.multiple_of(block * 32, 32), 32), 4 * LANES : 5 * LANES] = spread_stats(info)


def stats_kernel(pos, logits, target, send):
    for slot in range(3):
        fill_send(send, (pos[0] + OFFSETS[slot]) % 4, local_stats(logits[slot], target[slot]))


def near_stats(pos, logits, target):
    return pl.pallas_call(
        stats_kernel,
        in_specs=[SCALARS] + [WHOLE] * 2,
        out_specs=WHOLE,
        out_shape=jax.ShapeDtypeStruct((LANES, 5 * LANES), jnp.float32),
        compiler_params=params(),
        cost_estimate=cost(1000, 1000),
    )(pos, logits, target)


def last_kernel(pos, w, target, early, far_a, far_b, far_a2, far_b2, out, send, held):
    z, core = pos[0], pos[1]
    mine, other = core * 64, (1 - core) * 64
    for block, row in ((far_a, mine), (far_b, mine + 32), (far_a2, other), (far_b2, other + 32)):
        held[pl.ds(pl.multiple_of(row, 32), 32)] = block[...]
    out[...] = dot_nt(w[...], held[...])
    for block in range(5):
        at = slice(block * LANES, (block + 1) * LANES)
        send[:, at] = early[:, at]
    fill_send(send, (z + OFFSETS[3]) % 4, local_stats(out[...], target[3]))


def last_logits(pos, w, target, early, blocks):
    vocab, width = w.shape
    return pl.pallas_call(
        last_kernel,
        in_specs=[SCALARS] + [WHOLE] * 7,
        out_specs=[WHOLE] * 3,
        out_shape=[
            jax.ShapeDtypeStruct((vocab, LANES), jnp.float32),
            jax.ShapeDtypeStruct((LANES, 5 * LANES), jnp.float32),
            jax.ShapeDtypeStruct((LANES, width), jnp.bfloat16),
        ],
        compiler_params=params(),
        cost_estimate=cost(2 * vocab * width * 128, vocab * width * 2),
    )(pos, w, target, early, *blocks)


def grad_of(logits, lse, target):
    return loss_scale * (jnp.exp(logits - lse) - target)


def split_rows(pos, acc, at, base, mine_out, other_out):
    core = pos[1]
    mine_out[:, at] = acc[pl.ds(pl.multiple_of(base + core * 64, 64), 64)]
    other_out[:, at] = acc[pl.ds(pl.multiple_of(base + (1 - core) * 64, 64), 64)].astype(jnp.bfloat16)


def far_grad_kernel(pos, stats, logits, target, w, mine_out, other_out, grad_out, lse_out, loss_out, acc):
    z = pos[0]
    parts = stats[:, : 4 * LANES]
    peak = jnp.max(parts, axis=0, keepdims=True)
    lse = peak + jnp.log(jnp.sum(jnp.exp(parts - peak), axis=0, keepdims=True))
    for block in range(4):
        lse_out[block] = jnp.broadcast_to(lse[:, block * LANES : (block + 1) * LANES], (8, LANES))
    few = stats[:, 4 * LANES :]
    peak = jnp.max(few, axis=0, keepdims=True)
    weight = jnp.exp(few - peak)
    total = jnp.sum(weight, axis=0, keepdims=True)
    mean = jnp.sum(weight * pltpu.roll(few, LANES - 4, 1), axis=0, keepdims=True) / total
    cross = jnp.sum(pltpu.roll(few, LANES - 8, 1), axis=0, keepdims=True)
    lse4 = peak + jnp.log(total)
    row = lax.broadcasted_iota(jnp.int32, (8, LANES), 0)
    loss_out[...] = jnp.where(row == 0, lse4 - cross, lse4 - mean)
    far = lse_out[(z + OFFSETS[3]) % 4]
    grad = grad_of(logits[...], far[0:1], target[3])
    grad_out[...] = grad.astype(jnp.bfloat16)
    left = grad.T.astype(jnp.bfloat16)
    for tile in range(w.shape[1] // COLS):
        at = slice(tile * COLS, (tile + 1) * COLS)
        acc[...] = jnp.dot(left, w[:, at], preferred_element_type=jnp.float32)
        split_rows(pos, acc, at, 0, mine_out, other_out)


def far_grad(pos, stats, logits, target, w):
    vocab, width = w.shape
    return pl.pallas_call(
        far_grad_kernel,
        in_specs=[SCALARS] + [WHOLE] * 4,
        out_specs=[WHOLE] * 5,
        out_shape=[
            jax.ShapeDtypeStruct((64, width), jnp.float32),
            jax.ShapeDtypeStruct((64, width), jnp.bfloat16),
            jax.ShapeDtypeStruct((vocab, LANES), jnp.bfloat16),
            jax.ShapeDtypeStruct((4, 8, LANES), jnp.float32),
            jax.ShapeDtypeStruct((8, LANES), jnp.float32),
        ],
        scratch_shapes=[pltpu.VMEM((LANES, COLS), jnp.float32)],
        compiler_params=params(),
        cost_estimate=cost(2 * vocab * width * 128, vocab * width * 2),
    )(pos, stats, logits, target, w)


def grads_kernel(pos, logits, target, lse, far, wide_out, first_out, second_out, own_out):
    z = pos[0]
    for slot in range(3):
        row = lse[(z + OFFSETS[slot]) % 4]
        grad = grad_of(logits[slot], row[0:1], target[slot])
        wide_out[:, slot * LANES : (slot + 1) * LANES] = grad.astype(jnp.bfloat16)
        flipped = grad.T.astype(jnp.bfloat16)
        if slot == 0:
            own_out[...] = flipped
        else:
            for core in range(2):
                low = flipped[core * 64 : core * 64 + 32]
                high = flipped[core * 64 + 32 : core * 64 + 64]
                to = slice(core * 64 + (slot - 1) * 32, core * 64 + slot * 32)
                first_out[to, :] = low if slot == 1 else high
                second_out[to, :] = high if slot == 1 else low
    wide_out[:, 3 * LANES :] = far[...]


def near_grads(pos, logits, target, lse, far):
    vocab = far.shape[0]
    return pl.pallas_call(
        grads_kernel,
        in_specs=[SCALARS] + [WHOLE] * 4,
        out_specs=[WHOLE] * 4,
        out_shape=[jax.ShapeDtypeStruct((vocab, 4 * LANES), jnp.bfloat16)]
        + [jax.ShapeDtypeStruct((LANES, vocab), jnp.bfloat16)] * 3,
        compiler_params=params(),
        cost_estimate=cost(2e6, 5e6),
    )(pos, logits, target, lse, far)


def near_kernel(pos, left, w, mine_out, other_out, acc):
    core = pos[1]
    for tile in range(w.shape[1] // COLS):
        at = slice(tile * COLS, (tile + 1) * COLS)
        acc[...] = jnp.dot(left[...], w[:, at], preferred_element_type=jnp.float32)
        for slot in range(left.shape[0] // LANES):
            to = slice(slot * 64, (slot + 1) * 64)
            mine_out[to, at] = acc[pl.ds(pl.multiple_of(slot * 128 + core * 64, 64), 64)]
            part = acc[pl.ds(pl.multiple_of(slot * 128 + (1 - core) * 64, 64), 64)]
            other_out[to, at] = part.astype(jnp.bfloat16)


def near_grad(pos, left, w):
    vocab, width = w.shape
    tokens = left.shape[0]
    return pl.pallas_call(
        near_kernel,
        in_specs=[SCALARS] + [WHOLE] * 2,
        out_specs=[WHOLE] * 2,
        out_shape=[
            jax.ShapeDtypeStruct((tokens // 2, width), jnp.float32),
            jax.ShapeDtypeStruct((tokens // 2, width), jnp.bfloat16),
        ],
        scratch_shapes=[pltpu.VMEM((tokens, COLS), jnp.float32)],
        compiler_params=params(),
        cost_estimate=cost(2 * vocab * width * tokens, vocab * width * 2),
    )(pos, left, w)


def weight_kernel(grad, near, far, out):
    for tile in range(out.shape[1] // COLS):
        at = slice(tile * COLS, (tile + 1) * COLS)
        held = jnp.concatenate([near[:, at], far[:, at]], axis=0)
        out[:, at] = jnp.dot(grad[...], held, preferred_element_type=jnp.float32).astype(jnp.bfloat16)


def weight_grad(grad, near, far):
    vocab, tokens = grad.shape
    width = near.shape[1]
    rows = 256
    return pl.pallas_call(
        weight_kernel,
        grid=(vocab // rows,),
        in_specs=[pl.BlockSpec((rows, tokens), lambda i: (i, 0)), WHOLE, WHOLE],
        out_specs=pl.BlockSpec((rows, width), lambda i: (i, 0)),
        out_shape=jax.ShapeDtypeStruct((vocab, width), jnp.bfloat16),
        compiler_params=params(),
        cost_estimate=cost(2 * vocab * width * tokens, vocab * width * 2 + tokens * width * 2),
    )(grad, near, far)


def widen_kernel(upper, lower, out):
    out[0] = upper[...].astype(jnp.float32)
    out[1] = lower[...].astype(jnp.float32)


def widen(upper, lower):
    return pl.pallas_call(
        widen_kernel,
        in_specs=[WHOLE] * 2,
        out_specs=WHOLE,
        out_shape=jax.ShapeDtypeStruct((2, *upper.shape), jnp.float32),
        compiler_params=params(),
        cost_estimate=cost(1e11, 1e9),
    )(upper, lower)


def gather_own_kernel(mine, swap, left_b, right_b, out):
    half = left_b.shape[0]
    f32 = jnp.float32
    out[:half] = mine[:half] + swap[:half].astype(f32) + left_b[...].astype(f32)
    out[half:] = mine[half:] + swap[half:].astype(f32) + right_b[...].astype(f32)


def gather_own(*pieces):
    return pl.pallas_call(
        gather_own_kernel,
        in_specs=[WHOLE] * 4,
        out_specs=WHOLE,
        out_shape=jax.ShapeDtypeStruct(pieces[0].shape, jnp.float32),
        compiler_params=params(),
        cost_estimate=cost(1e11, 1e9),
    )(*pieces)


def fold_kernel(near, right_a, left_a, out, total):
    half = right_a.shape[0]
    total[:half] = (near[:half] + right_a[...].astype(jnp.float32)).astype(jnp.bfloat16)
    total[half:] = (near[half:] + left_a[...].astype(jnp.float32)).astype(jnp.bfloat16)
    part = out.shape[2]
    for index in range(out.shape[0]):
        out[index] = total[:, index * part : (index + 1) * part]


def fold(count, pieces):
    rows, width = pieces[0].shape
    return pl.pallas_call(
        fold_kernel,
        in_specs=[WHOLE] * 3,
        out_specs=WHOLE,
        out_shape=jax.ShapeDtypeStruct((count, rows, width // count), jnp.bfloat16),
        scratch_shapes=[pltpu.VMEM((rows, width), jnp.bfloat16)],
        compiler_params=params(),
        cost_estimate=cost(2e6, 4e6),
    )(*pieces)


def sum_kernel(parts, out):
    total = parts[0].astype(jnp.float32)
    for index in range(1, parts.shape[0]):
        total = total + parts[index].astype(jnp.float32)
    out[...] = total.astype(jnp.bfloat16)


def sum_parts(parts):
    return pl.pallas_call(
        sum_kernel,
        in_specs=[WHOLE],
        out_specs=WHOLE,
        out_shape=jax.ShapeDtypeStruct(parts.shape[1:], jnp.bfloat16),
        compiler_params=params(),
        cost_estimate=cost(4e5, 8e5),
    )(parts)


def body(hidden, head_weight, teacher_logits, teacher_ids):
    seq_count = lax.axis_size("seq")
    vocab_count = lax.axis_size("vocab")
    owners = seq_count * vocab_count
    vocab_rows, width = head_weight.shape
    tok_rows, feat_part = hidden.shape
    seq_index = lax.axis_index("seq")
    pos = jnp.stack([seq_index // 2, seq_index % 2]).astype(jnp.int32)
    up = [(i, (i + 2) % seq_count) for i in range(seq_count)]
    down = [(i, (i - 2) % seq_count) for i in range(seq_count)]
    twin = [(i, i ^ 1) for i in range(seq_count)]

    def move(x, perm):
        return lax.ppermute(x, "seq", perm)

    def after(x, *before):
        return lax.optimization_barrier((x, before))[0]

    f32 = jnp.float32
    bf16 = jnp.bfloat16
    half = tok_rows // 2

    hidden, pos = lax.optimization_barrier((hidden, pos))
    spread = copies_of(hidden, vocab_count)
    spread = lax.all_to_all(spread, "vocab", split_axis=0, concat_axis=0, tiled=True)
    own = join_parts(spread)
    left = move(own, up)
    right = move(own, down)
    own2 = move(own, twin)
    teacher_logits, own = lax.optimization_barrier((teacher_logits, own))
    teach = teacher_rows(owners, vocab_rows, teacher_logits, teacher_ids)
    got = lax.all_to_all(teach, BOTH, split_axis=0, concat_axis=0, tiled=True)
    left, right = after((left, right), got)
    far_a = move(left[:half], up)
    far_b = move(right[half:], down)
    near_blocks = (own, own2, left, move(left, twin), right, move(right, twin))
    weight, logits, target, near_rows = first_logits(pos, got, head_weight, near_blocks)
    far_a, far_b = after((far_a, far_b), logits)
    early = near_stats(pos, logits, target)
    far_blocks = (far_a, far_b, move(far_a, twin), move(far_b, twin))
    far_logits, send, far_rows = last_logits(pos, weight, target, early, far_blocks)
    stats = lax.all_to_all(send, BOTH, split_axis=0, concat_axis=0, tiled=True)

    far_mine, far_other, grad_far, lse, loss = far_grad(pos, stats, far_logits, target, weight)
    far_swap = move(far_other, twin)
    wide, first_left, second_left, own_left = near_grads(pos, logits, target, lse, grad_far)
    first_mine, first_other = near_grad(pos, first_left, weight)
    first_swap = move(first_other, twin)
    far_sum = (far_mine + far_swap.astype(f32)).astype(bf16)
    go_up = move(far_sum[:half], up)
    go_down = move(far_sum[half:], down)
    second_left = after(second_left, far_sum, first_other)
    second_mine, second_other = near_grad(pos, second_left, weight)
    second_swap = move(second_other, twin)
    own_left = after(own_left, second_other)
    own_mine, own_other = near_grad(pos, own_left, weight)
    own_swap = move(own_other, twin)
    first_sum = (first_mine + first_swap.astype(f32)).astype(bf16)
    left_b_part, right_b_part = first_sum[:half], first_sum[half:]
    left_b = move(left_b_part, down)
    right_b = move(right_b_part, up)
    second_sum = second_mine + second_swap.astype(f32)
    go_up, go_down = after((go_up, go_down), right_b_part, left_b_part)
    passed = widen(go_up, go_down)
    left_a_part = (second_sum[:half] + passed[1]).astype(bf16)
    right_a_part = (second_sum[half:] + passed[0]).astype(bf16)
    left_a = move(left_a_part, down)
    right_a = move(right_a_part, up)
    grad_weight = weight_grad(after(wide, left_a_part, right_a_part), near_rows, far_rows)
    left_b, right_b = after((left_b, right_b), grad_weight)
    gathered = gather_own(own_mine, own_swap, left_b, right_b)
    (right_a, left_a), gathered = lax.optimization_barrier(((right_a, left_a), gathered))
    parts = fold(vocab_count, (gathered, right_a, left_a))
    parts = lax.all_to_all(parts, "vocab", split_axis=0, concat_axis=0, tiled=True)
    grad_hidden = sum_parts(parts)
    rows = teacher_logits.shape[0]
    return loss[0, :rows], loss[1, :rows], grad_hidden, grad_weight


def solution(mesh):
    placed = (
        P("seq", "vocab"),
        P(("seq", "vocab"), None),
        P(("seq", "vocab"), None),
        P(("seq", "vocab"), None),
    )
    return jax.shard_map(
        body,
        mesh=mesh,
        in_specs=placed,
        out_specs=(
            P(("seq", "vocab")),
            P(("seq", "vocab")),
            P("seq", "vocab"),
            P(("seq", "vocab"), None),
        ),
        check_vma=False,
    )
```

```python
import functools

import jax
import jax.numpy as jnp
from jax import lax
from jax.experimental import pallas as pl
from jax.experimental.pallas import tpu as pltpu
from jax.sharding import PartitionSpec as P

loss_scale = 64.0
SLOTS = 6
LANES = 128
COLS = 768
ANY = pl.BlockSpec(memory_space=pl.ANY)
WHOLE = pl.BlockSpec(memory_space=pltpu.VMEM)
FAR = pl.BlockSpec(memory_space=pltpu.HBM)
SCALARS = pl.BlockSpec(memory_space=pltpu.SMEM)
VMEM_LIMIT = 16 * 1024 * 1024
BOTH = ("seq", "vocab")


def plane(pos, slot):
    z, core = pos[0], pos[1]
    return (z + (0, 3 - 2 * core, 1 + 2 * core, 2)[slot]) % 4


def params():
    return pltpu.CompilerParams(vmem_limit_bytes=VMEM_LIMIT)


def cost(flops, nbytes):
    return pl.CostEstimate(flops=int(flops), bytes_accessed=int(nbytes), transcendentals=0)


def teacher_kernel(owners, vocab_rows, logits_ref, ids_ref, out_ref):
    rows, width = logits_ref.shape
    scores = logits_ref[...]
    expo = jnp.exp(scores - jnp.max(scores, axis=1, keepdims=True))
    prob = expo / jnp.sum(expo, axis=1, keepdims=True)
    ids = ids_ref[...]
    shift = vocab_rows.bit_length() - 1
    owner_of = lax.shift_right_logical(ids, shift)
    local_of = (ids - owner_of * vocab_rows + 1).astype(jnp.float32)
    owner_of = owner_of.astype(jnp.float32)
    owner_iota = lax.broadcasted_iota(jnp.int32, (owners, width), 0).astype(jnp.float32)
    slot_iota = lax.broadcasted_iota(jnp.int32, (owners, width), 1).astype(jnp.float32)
    lane = lax.broadcasted_iota(jnp.int32, (owners, rows * 16), 1)
    out = jnp.zeros((owners, rows * 16), jnp.float32)
    for row in range(rows):
        row_prob = jnp.broadcast_to(prob[row : row + 1, :], (owners, width))
        owner = jnp.broadcast_to(owner_of[row : row + 1, :], (owners, width))
        local = jnp.broadcast_to(local_of[row : row + 1, :], (owners, width))
        same = owner == owner_iota
        start = jnp.sum(jnp.where(owner < owner_iota, 1.0, 0.0), axis=1, keepdims=True)
        place = jnp.where(same, slot_iota - start, -1.0)
        for slot in range(2):
            hit = place == slot
            value = jnp.sum(jnp.where(hit, row_prob, 0.0), axis=1, keepdims=True)
            index = jnp.sum(jnp.where(hit, local, 0.0), axis=1, keepdims=True) - 1.0
            out = out + jnp.where(lane == row * 16 + slot, value, jnp.where(lane == row * 16 + 8 + slot, index, 0.0))
        many = jnp.sum(jnp.where(same, 1.0, 0.0), axis=1, keepdims=True) > 2.0
        first = jnp.sum(jnp.where(many, start, 0.0), axis=0, keepdims=True)
        hot_place = slot_iota[:1] - first
        hot_index = local_of[row : row + 1, :]
        extra = jnp.zeros((1, rows * 16), jnp.float32)
        for slot in range(2, SLOTS):
            hit = hot_place == slot
            value = jnp.sum(jnp.where(hit, prob[row : row + 1, :], 0.0), axis=1, keepdims=True)
            index = jnp.sum(jnp.where(hit, hot_index, 0.0), axis=1, keepdims=True)
            at = lane[:1]
            extra = extra + jnp.where(at == row * 16 + slot, value, jnp.where(at == row * 16 + 8 + slot, index, 0.0))
        empty = (lane >= row * 16 + 10) & (lane < row * 16 + 8 + SLOTS)
        out = out + jnp.where(many, extra, 0.0) - empty.astype(jnp.float32)
    out_ref[...] = out


def teacher_rows(owners, vocab_rows, teacher_logits, teacher_ids):
    rows = teacher_logits.shape[0]
    return pl.pallas_call(
        functools.partial(teacher_kernel, owners, vocab_rows),
        out_shape=jax.ShapeDtypeStruct((owners, rows * 16), jnp.float32),
        compiler_params=params(),
        cost_estimate=cost(4e6, 40000),
    )(teacher_logits, teacher_ids)


def copies_kernel(block, out):
    for index in range(out.shape[0]):
        out[index] = block[...]


def copies_of(block, count):
    return pl.pallas_call(
        copies_kernel,
        in_specs=[WHOLE],
        out_specs=WHOLE,
        out_shape=jax.ShapeDtypeStruct((count, *block.shape), block.dtype),
        compiler_params=params(),
        cost_estimate=cost(1000, 1e6),
    )(block)


def join_kernel(parts, out, rows):
    part = parts.shape[2]
    for index in range(parts.shape[0]):
        rows[:, index * part : (index + 1) * part] = parts[index].astype(jnp.float32)
    out[...] = rows[...].astype(jnp.bfloat16)


def join_parts(parts):
    count, rows, part = parts.shape
    return pl.pallas_call(
        join_kernel,
        in_specs=[WHOLE],
        out_specs=WHOLE,
        out_shape=jax.ShapeDtypeStruct((rows, count * part), parts.dtype),
        scratch_shapes=[pltpu.VMEM((rows, count * part), jnp.float32)],
        compiler_params=params(),
        cost_estimate=cost(1e6, 2e6),
    )(parts)


def dot_nt(a, b):
    return lax.dot_general(a, b, (((1,), (1,)), ((), ())), preferred_element_type=jnp.float32)


def local_stats(logits, target):
    peak = jnp.max(logits, axis=0, keepdims=True)
    expo = jnp.exp(logits - peak)
    total = jnp.sum(expo, axis=0, keepdims=True)
    mean = jnp.sum(expo * logits, axis=0, keepdims=True) / total
    cross = jnp.sum(target * logits, axis=0, keepdims=True)
    lse = peak + jnp.log(total)
    row = lax.broadcasted_iota(jnp.int32, (8, LANES), 0)
    return jnp.where(row == 0, lse, jnp.where(row == 1, mean, jnp.where(row == 2, cross, 0.0)))


def first_kernel(pos, got, source, own, own2, next1, next2, w, out, target, held, teach, sems):
    core = pos[1]
    pieces = (slice(0, 1024),)
    copies = [
        pltpu.make_async_copy(
            source.at[pl.ds(at.start, at.stop - at.start)], w.at[pl.ds(at.start, at.stop - at.start)], sems.at[k]
        )
        for k, at in enumerate(pieces)
    ]
    copies[0].start()
    mine, other = core * 64, (1 - core) * 64
    for block, row in ((own, mine), (own2, other), (next1, 128 + mine), (next2, 128 + other)):
        held[pl.ds(pl.multiple_of(row, 64), 64)] = block[...]
    flipped = got[...].T
    source_row = lax.broadcasted_iota(jnp.int32, (LANES, 4 * LANES), 0)
    token = lax.broadcasted_iota(jnp.int32, (LANES, 4 * LANES), 1)
    spread = jnp.zeros((16, 4 * LANES), jnp.float32)
    for row in range(4):
        pick = (token == source_row * 4 + row).astype(jnp.float32)
        spread = spread + jnp.dot(
            flipped[row * 16 : row * 16 + 16], pick,
            precision=lax.Precision.HIGHEST, preferred_element_type=jnp.float32,
        )
    for block in range(4):
        teach[block] = spread[:, block * LANES : (block + 1) * LANES]
    rows = 32
    low_iota = lax.broadcasted_iota(jnp.int32, (rows, LANES), 0).astype(jnp.float32)
    for slot in range(4):
        info = teach[plane(pos, slot)]
        groups, values = [], []
        for k in range(SLOTS):
            index = info[8 + k : 9 + k]
            group = jnp.floor(index * (1.0 / rows))
            groups.append(group)
            values.append(jnp.where(low_iota == index - group * rows, info[k : k + 1], 0.0))

        @pl.loop(0, w.shape[0] // rows, unroll=4)
        def _(step):
            number = jnp.full((1, LANES), step, jnp.int32).astype(jnp.float32)
            dense = jnp.zeros((rows, LANES), jnp.float32)
            for group, value in zip(groups, values):
                dense = dense + jnp.where(group == number, value, 0.0)
            target[slot, pl.ds(pl.multiple_of(step * rows, rows), rows)] = dense

    for k, at in enumerate(pieces):
        copies[k].wait()
        if k + 1 < len(pieces):
            copies[k + 1].start()
        logits = dot_nt(w[at], held[...])
        for slot in range(2):
            out[slot, at] = logits[:, slot * LANES : (slot + 1) * LANES]


def first_logits(pos, got, source, blocks):
    vocab, width = source.shape
    return pl.pallas_call(
        first_kernel,
        in_specs=[SCALARS, WHOLE, FAR] + [WHOLE] * 4,
        out_specs=[WHOLE] * 4,
        out_shape=[
            pltpu.VMEM((vocab, width), jnp.bfloat16),
            jax.ShapeDtypeStruct((2, vocab, LANES), jnp.float32),
            jax.ShapeDtypeStruct((4, vocab, LANES), jnp.float32),
            jax.ShapeDtypeStruct((2 * LANES, width), jnp.bfloat16),
        ],
        scratch_shapes=[pltpu.VMEM((4, 16, LANES), jnp.float32), pltpu.SemaphoreType.DMA((1,))],
        compiler_params=params(),
        cost_estimate=cost(1e11, 1e9),
    )(pos, got, pltpu.with_memory_space_constraint(source, pltpu.HBM), *blocks)


def spread_stats(info):
    lane = lax.broadcasted_iota(jnp.int32, (32, LANES), 1)
    row = lax.broadcasted_iota(jnp.int32, (32, LANES), 0)
    extra = jnp.zeros((32, LANES), jnp.float32)
    for kind in range(3):
        for token in range(4):
            value = jnp.sum(jnp.where(lane == row * 4 + token, info[kind : kind + 1], 0.0), axis=1, keepdims=True)
            extra = extra + jnp.where(lane == kind * 4 + token, value, 0.0)
    return extra


def fill_send(send, block, info):
    send[:, pl.ds(pl.multiple_of(block * LANES, LANES), LANES)] = jnp.broadcast_to(info[0:1], (LANES, LANES))
    send[pl.ds(pl.multiple_of(block * 32, 32), 32), 4 * LANES : 5 * LANES] = spread_stats(info)


def stats_kernel(pos, logits, target, send):
    for slot in range(2):
        fill_send(send, plane(pos, slot), local_stats(logits[slot], target[slot]))


def near_stats(pos, logits, target):
    return pl.pallas_call(
        stats_kernel,
        in_specs=[SCALARS] + [WHOLE] * 2,
        out_specs=WHOLE,
        out_shape=jax.ShapeDtypeStruct((LANES, 5 * LANES), jnp.float32),
        compiler_params=params(),
        cost_estimate=cost(1000, 1000),
    )(pos, logits, target)


def last_kernel(pos, w, target, early, back1, back2, far, far2, out, send, held):
    core = pos[1]
    mine, other = core * 64, (1 - core) * 64
    for block, row in ((back1, other), (back2, mine), (far, 128 + mine), (far2, 128 + other)):
        held[pl.ds(pl.multiple_of(row, 64), 64)] = block[...]
    logits = dot_nt(w[...], held[...])
    for block in range(5):
        at = slice(block * LANES, (block + 1) * LANES)
        send[:, at] = early[:, at]
    for slot in range(2):
        out[slot] = logits[:, slot * LANES : (slot + 1) * LANES]
    for slot in range(2):
        fill_send(send, plane(pos, 2 + slot), local_stats(out[slot], target[2 + slot]))


def last_logits(pos, w, target, early, blocks):
    vocab, width = w.shape
    return pl.pallas_call(
        last_kernel,
        in_specs=[SCALARS] + [WHOLE] * 7,
        out_specs=[WHOLE] * 3,
        out_shape=[
            jax.ShapeDtypeStruct((2, vocab, LANES), jnp.float32),
            jax.ShapeDtypeStruct((LANES, 5 * LANES), jnp.float32),
            jax.ShapeDtypeStruct((2 * LANES, width), jnp.bfloat16),
        ],
        compiler_params=params(),
        cost_estimate=cost(2 * vocab * width * 256, vocab * width * 2),
    )(pos, w, target, early, *blocks)


def grad_of(logits, lse, target):
    return loss_scale * (jnp.exp(logits - lse) - target)


def split_dot(left, w, mine_out, other_out):
    for tile in range(w.shape[1] // COLS):
        at = slice(tile * COLS, (tile + 1) * COLS)
        grad = jnp.dot(left[...], w[:, at], preferred_element_type=jnp.float32)
        for slot in range(left.shape[0] // LANES):
            to, base = slice(slot * 64, (slot + 1) * 64), slot * LANES
            mine_out[to, at] = grad[base : base + 64]
            other_out[to, at] = grad[base + 64 : base + LANES].astype(jnp.bfloat16)


def far_grad_kernel(pos, stats, logits, target, w, mine_out, other_out, grad_out, lse_out, loss_out, flipped, left):
    parts = stats[:, : 4 * LANES]
    peak = jnp.max(parts, axis=0, keepdims=True)
    lse = peak + jnp.log(jnp.sum(jnp.exp(parts - peak), axis=0, keepdims=True))
    for block in range(4):
        lse_out[block] = jnp.broadcast_to(lse[:, block * LANES : (block + 1) * LANES], (8, LANES))
    few = stats[:, 4 * LANES :]
    peak = jnp.max(few, axis=0, keepdims=True)
    weight = jnp.exp(few - peak)
    total = jnp.sum(weight, axis=0, keepdims=True)
    mean = jnp.sum(weight * pltpu.roll(few, LANES - 4, 1), axis=0, keepdims=True) / total
    cross = jnp.sum(pltpu.roll(few, LANES - 8, 1), axis=0, keepdims=True)
    lse4 = peak + jnp.log(total)
    row = lax.broadcasted_iota(jnp.int32, (8, LANES), 0)
    loss_out[...] = jnp.where(row == 0, lse4 - cross, lse4 - mean)
    far = lse_out[plane(pos, 3)]
    grad = grad_of(logits[1], far[0:1], target[3])
    grad_out[...] = grad.astype(jnp.bfloat16)
    core = pos[1]
    flipped[...] = grad.T.astype(jnp.bfloat16)
    left[:64, :] = flipped[pl.ds(pl.multiple_of(core * 64, 64), 64)]
    left[64:, :] = flipped[pl.ds(pl.multiple_of((1 - core) * 64, 64), 64)]
    split_dot(left, w, mine_out, other_out)


def far_grad(pos, stats, logits, target, w):
    vocab, width = w.shape
    return pl.pallas_call(
        far_grad_kernel,
        in_specs=[SCALARS] + [WHOLE] * 4,
        out_specs=[WHOLE] * 5,
        out_shape=[
            jax.ShapeDtypeStruct((64, width), jnp.float32),
            jax.ShapeDtypeStruct((64, width), jnp.bfloat16),
            jax.ShapeDtypeStruct((vocab, LANES), jnp.bfloat16),
            jax.ShapeDtypeStruct((4, 8, LANES), jnp.float32),
            jax.ShapeDtypeStruct((8, LANES), jnp.float32),
        ],
        scratch_shapes=[pltpu.VMEM((LANES, vocab), jnp.bfloat16)] * 2,
        compiler_params=params(),
        cost_estimate=cost(2 * vocab * width * 128, vocab * width * 2),
    )(pos, stats, logits, target, w)


def grads_kernel(pos, logits, last, target, lse, far, wide_out, first_out, second_out, flipped):
    core = pos[1]
    mine, other = pl.ds(pl.multiple_of(core * 64, 64), 64), pl.ds(pl.multiple_of((1 - core) * 64, 64), 64)
    for slot in (2, 1, 0):
        part = last[0] if slot == 2 else logits[slot]
        grad = grad_of(part, lse[plane(pos, slot)][0:1], target[slot])
        wide_out[:, slot * LANES : (slot + 1) * LANES] = grad.astype(jnp.bfloat16)
        flipped[...] = grad.T.astype(jnp.bfloat16)
        if slot == 2:
            first_out[:64, :] = flipped[other]
            second_out[:64, :] = flipped[mine]
        elif slot == 1:
            first_out[64:, :] = flipped[mine]
            second_out[64:128, :] = flipped[other]
        else:
            second_out[128:192, :] = flipped[mine]
            second_out[192:, :] = flipped[other]
    wide_out[:, 3 * LANES :] = far[...]


def near_grads(pos, logits, last, target, lse, far):
    vocab = far.shape[0]
    return pl.pallas_call(
        grads_kernel,
        in_specs=[SCALARS] + [WHOLE] * 5,
        out_specs=[WHOLE] * 3,
        out_shape=[
            jax.ShapeDtypeStruct((vocab, 4 * LANES), jnp.bfloat16),
            jax.ShapeDtypeStruct((LANES, vocab), jnp.bfloat16),
            jax.ShapeDtypeStruct((2 * LANES, vocab), jnp.bfloat16),
        ],
        scratch_shapes=[pltpu.VMEM((LANES, vocab), jnp.bfloat16)],
        compiler_params=params(),
        cost_estimate=cost(2e6, 5e6),
    )(pos, logits, last, target, lse, far)


def near_kernel(left, w, mine_out, other_out):
    split_dot(left, w, mine_out, other_out)


def near_grad(left, w):
    vocab, width = w.shape
    tokens = left.shape[0]
    return pl.pallas_call(
        near_kernel,
        in_specs=[WHOLE] * 2,
        out_specs=[WHOLE] * 2,
        out_shape=[
            jax.ShapeDtypeStruct((tokens // 2, width), jnp.float32),
            jax.ShapeDtypeStruct((tokens // 2, width), jnp.bfloat16),
        ],
        compiler_params=params(),
        cost_estimate=cost(2 * vocab * width * tokens, vocab * width * 2),
    )(left, w)


def weight_kernel(grad, near, far, out):
    for tile in range(out.shape[1] // COLS):
        at = slice(tile * COLS, (tile + 1) * COLS)
        held = jnp.concatenate([near[:, at], far[:, at]], axis=0)
        out[:, at] = jnp.dot(grad[...], held, preferred_element_type=jnp.float32).astype(jnp.bfloat16)


def weight_grad(grad, near, far):
    vocab, tokens = grad.shape
    width = near.shape[1]
    rows = 256
    return pl.pallas_call(
        weight_kernel,
        grid=(vocab // rows,),
        in_specs=[pl.BlockSpec((rows, tokens), lambda i: (i, 0)), WHOLE, WHOLE],
        out_specs=pl.BlockSpec((rows, width), lambda i: (i, 0)),
        out_shape=jax.ShapeDtypeStruct((vocab, width), jnp.bfloat16),
        compiler_params=params(),
        cost_estimate=cost(2 * vocab * width * tokens, vocab * width * 2 + tokens * width * 2),
    )(grad, near, far)


def widen_kernel(block, out):
    out[...] = block[...].astype(jnp.float32)


def widen(block):
    return pl.pallas_call(
        widen_kernel,
        in_specs=[WHOLE],
        out_specs=WHOLE,
        out_shape=jax.ShapeDtypeStruct(block.shape, jnp.float32),
        compiler_params=params(),
        cost_estimate=cost(1e11, 1e9),
    )(block)


def gather_own_kernel(mine, swap, across, out):
    rows = out.shape[0]
    f32 = jnp.float32
    out[...] = mine[rows:] + swap[rows:].astype(f32) + across[...].astype(f32)


def gather_own(mine, swap, across):
    return pl.pallas_call(
        gather_own_kernel,
        in_specs=[WHOLE] * 3,
        out_specs=WHOLE,
        out_shape=jax.ShapeDtypeStruct(across.shape, jnp.float32),
        compiler_params=params(),
        cost_estimate=cost(1e11, 1e9),
    )(mine, swap, across)


def fold_kernel(near, arrived, out, total):
    total[...] = (near[...] + arrived[...].astype(jnp.float32)).astype(jnp.bfloat16)
    part = out.shape[2]
    for index in range(out.shape[0]):
        out[index] = total[:, index * part : (index + 1) * part]


def fold(count, near, arrived):
    rows, width = near.shape
    return pl.pallas_call(
        fold_kernel,
        in_specs=[WHOLE] * 2,
        out_specs=WHOLE,
        out_shape=jax.ShapeDtypeStruct((count, rows, width // count), jnp.bfloat16),
        scratch_shapes=[pltpu.VMEM((rows, width), jnp.bfloat16)],
        compiler_params=params(),
        cost_estimate=cost(2e6, 4e6),
    )(near, arrived)


def sum_kernel(parts, out):
    total = parts[0].astype(jnp.float32)
    for index in range(1, parts.shape[0]):
        total = total + parts[index].astype(jnp.float32)
    out[...] = total.astype(jnp.bfloat16)


def sum_parts(parts):
    return pl.pallas_call(
        sum_kernel,
        in_specs=[WHOLE],
        out_specs=WHOLE,
        out_shape=jax.ShapeDtypeStruct(parts.shape[1:], jnp.bfloat16),
        compiler_params=params(),
        cost_estimate=cost(4e5, 8e5),
    )(parts)


def body(hidden, head_weight, teacher_logits, teacher_ids):
    seq_count = lax.axis_size("seq")
    vocab_count = lax.axis_size("vocab")
    owners = seq_count * vocab_count
    vocab_rows, width = head_weight.shape
    tok_rows, feat_part = hidden.shape
    seq_index = lax.axis_index("seq")
    pos = jnp.stack([seq_index // 2, seq_index % 2]).astype(jnp.int32)
    ring = [(i, (i + 2 - 4 * (i % 2)) % seq_count) for i in range(seq_count)]
    cross = [(i, (i + 2 - 4 * (i % 2)) % seq_count ^ 1) for i in range(seq_count)]
    twin = [(i, i ^ 1) for i in range(seq_count)]

    def move(x, perm):
        return lax.ppermute(x, "seq", perm)

    def after(x, *before):
        return lax.optimization_barrier((x, before))[0]

    f32 = jnp.float32
    bf16 = jnp.bfloat16

    hidden, pos = lax.optimization_barrier((hidden, pos))
    spread = copies_of(hidden, vocab_count)
    spread = lax.all_to_all(spread, "vocab", split_axis=0, concat_axis=0, tiled=True)
    own = join_parts(spread)
    next1 = move(own, ring)
    own2 = move(own, twin)
    next2 = move(own2, ring)
    teacher_logits, own2 = lax.optimization_barrier((teacher_logits, own2))
    teach = teacher_rows(owners, vocab_rows, teacher_logits, teacher_ids)
    got = lax.all_to_all(teach, BOTH, split_axis=0, concat_axis=0, tiled=True)
    far = move(next1, ring)
    near_blocks = (own, own2, next1, next2)
    weight, logits, target, near_rows = first_logits(pos, got, head_weight, near_blocks)
    back = (move(next1, twin), move(next2, twin))
    far = after(far, logits)
    early = near_stats(pos, logits, target)
    last, send, last_rows = last_logits(pos, weight, target, early, (*back, far, move(far, twin)))
    stats = lax.all_to_all(send, BOTH, split_axis=0, concat_axis=0, tiled=True)

    far_mine, far_other, grad_far, lse, loss = far_grad(pos, stats, last, target, weight)
    far_swap = move(far_other, twin)
    wide, first_left, second_left = near_grads(pos, logits, last, target, lse, grad_far)
    first_mine, first_other = near_grad(first_left, weight)
    first_swap = move(first_other, twin)
    far_sum = (far_mine + far_swap.astype(f32)).astype(bf16)
    passed = move(far_sum, ring)
    second_left = after(second_left, far_sum, first_other)
    second_mine, second_other = near_grad(second_left, weight)
    second_swap = move(second_other, twin)
    first_sum = (first_mine + first_swap.astype(f32)).astype(bf16)
    first = move(first_sum, cross)
    passed = widen(after(passed, first_sum))
    second_sum = second_mine[:tok_rows] + second_swap[:tok_rows].astype(f32)
    second_sum = (second_sum + passed).astype(bf16)
    second = move(second_sum, ring)
    rows = teacher_logits.shape[0]
    loss = after(loss, second_sum)
    cross_entropy, entropy = loss[0, :rows], loss[1, :rows]
    wide = after(wide, second_sum, cross_entropy, entropy)
    grad_weight = weight_grad(wide, near_rows, last_rows)
    first = after(first, grad_weight)
    gathered = gather_own(second_mine, second_swap, first)
    second, gathered = lax.optimization_barrier((second, gathered))
    parts = fold(vocab_count, gathered, second)
    parts = lax.all_to_all(parts, "vocab", split_axis=0, concat_axis=0, tiled=True)
    grad_hidden = sum_parts(parts)
    return cross_entropy, entropy, grad_hidden, grad_weight


def solution(mesh):
    placed = (
        P("seq", "vocab"),
        P(("seq", "vocab"), None),
        P(("seq", "vocab"), None),
        P(("seq", "vocab"), None),
    )
    return jax.shard_map(
        body,
        mesh=mesh,
        in_specs=placed,
        out_specs=(
            P(("seq", "vocab")),
            P(("seq", "vocab")),
            P("seq", "vocab"),
            P(("seq", "vocab"), None),
        ),
        check_vma=False,
    )
```

```python
import functools

import jax
import jax.numpy as jnp
from jax import lax
from jax.experimental import pallas as pl
from jax.experimental.pallas import tpu as pltpu
from jax.sharding import PartitionSpec as P

loss_scale = 64.0
SLOTS = 6
LANES = 128
COLS = 768
ANY = pl.BlockSpec(memory_space=pl.ANY)
WHOLE = pl.BlockSpec(memory_space=pltpu.VMEM)
FAR = pl.BlockSpec(memory_space=pltpu.HBM)
SCALARS = pl.BlockSpec(memory_space=pltpu.SMEM)
VMEM_LIMIT = 16 * 1024 * 1024
BOTH = ("seq", "vocab")


def plane(pos, slot):
    z, core = pos[0], pos[1]
    return (z + (0, 3 - 2 * core, 1 + 2 * core, 2)[slot]) % 4


def params():
    return pltpu.CompilerParams(vmem_limit_bytes=VMEM_LIMIT)


def cost(flops, nbytes):
    return pl.CostEstimate(flops=int(flops), bytes_accessed=int(nbytes), transcendentals=0)


def teacher_kernel(owners, vocab_rows, logits_ref, ids_ref, out_ref):
    rows, width = logits_ref.shape
    scores = logits_ref[...]
    expo = jnp.exp(scores - jnp.max(scores, axis=1, keepdims=True))
    prob = expo / jnp.sum(expo, axis=1, keepdims=True)
    ids = ids_ref[...]
    shift = vocab_rows.bit_length() - 1
    owner_of = lax.shift_right_logical(ids, shift)
    local_of = (ids - owner_of * vocab_rows + 1).astype(jnp.float32)
    owner_of = owner_of.astype(jnp.float32)
    owner_iota = lax.broadcasted_iota(jnp.int32, (owners, width), 0).astype(jnp.float32)
    slot_iota = lax.broadcasted_iota(jnp.int32, (owners, width), 1).astype(jnp.float32)
    lane = lax.broadcasted_iota(jnp.int32, (owners, rows * 16), 1)
    out = jnp.zeros((owners, rows * 16), jnp.float32)
    for row in range(rows):
        row_prob = jnp.broadcast_to(prob[row : row + 1, :], (owners, width))
        owner = jnp.broadcast_to(owner_of[row : row + 1, :], (owners, width))
        local = jnp.broadcast_to(local_of[row : row + 1, :], (owners, width))
        same = owner == owner_iota
        start = jnp.sum(jnp.where(owner < owner_iota, 1.0, 0.0), axis=1, keepdims=True)
        place = jnp.where(same, slot_iota - start, -1.0)
        for slot in range(2):
            hit = place == slot
            value = jnp.sum(jnp.where(hit, row_prob, 0.0), axis=1, keepdims=True)
            index = jnp.sum(jnp.where(hit, local, 0.0), axis=1, keepdims=True) - 1.0
            out = out + jnp.where(lane == row * 16 + slot, value, jnp.where(lane == row * 16 + 8 + slot, index, 0.0))
        many = jnp.sum(jnp.where(same, 1.0, 0.0), axis=1, keepdims=True) > 2.0
        first = jnp.sum(jnp.where(many, start, 0.0), axis=0, keepdims=True)
        hot_place = slot_iota[:1] - first
        hot_index = local_of[row : row + 1, :]
        extra = jnp.zeros((1, rows * 16), jnp.float32)
        for slot in range(2, SLOTS):
            hit = hot_place == slot
            value = jnp.sum(jnp.where(hit, prob[row : row + 1, :], 0.0), axis=1, keepdims=True)
            index = jnp.sum(jnp.where(hit, hot_index, 0.0), axis=1, keepdims=True)
            at = lane[:1]
            extra = extra + jnp.where(at == row * 16 + slot, value, jnp.where(at == row * 16 + 8 + slot, index, 0.0))
        empty = (lane >= row * 16 + 10) & (lane < row * 16 + 8 + SLOTS)
        out = out + jnp.where(many, extra, 0.0) - empty.astype(jnp.float32)
    out_ref[...] = out


def teacher_rows(owners, vocab_rows, teacher_logits, teacher_ids):
    rows = teacher_logits.shape[0]
    return pl.pallas_call(
        functools.partial(teacher_kernel, owners, vocab_rows),
        out_shape=jax.ShapeDtypeStruct((owners, rows * 16), jnp.float32),
        compiler_params=params(),
        cost_estimate=cost(4e6, 40000),
    )(teacher_logits, teacher_ids)


def copies_kernel(block, out):
    for index in range(out.shape[0]):
        out[index] = block[...]


def copies_of(block, count):
    return pl.pallas_call(
        copies_kernel,
        in_specs=[WHOLE],
        out_specs=WHOLE,
        out_shape=jax.ShapeDtypeStruct((count, *block.shape), block.dtype),
        compiler_params=params(),
        cost_estimate=cost(1000, 1e6),
    )(block)


def join_kernel(parts, out, rows):
    part = parts.shape[2]
    for index in range(parts.shape[0]):
        rows[:, index * part : (index + 1) * part] = parts[index].astype(jnp.float32)
    out[...] = rows[...].astype(jnp.bfloat16)


def join_parts(parts):
    count, rows, part = parts.shape
    return pl.pallas_call(
        join_kernel,
        in_specs=[WHOLE],
        out_specs=WHOLE,
        out_shape=jax.ShapeDtypeStruct((rows, count * part), parts.dtype),
        scratch_shapes=[pltpu.VMEM((rows, count * part), jnp.float32)],
        compiler_params=params(),
        cost_estimate=cost(1e6, 2e6),
    )(parts)


def dot_nt(a, b):
    return lax.dot_general(a, b, (((1,), (1,)), ((), ())), preferred_element_type=jnp.float32)


def local_stats(logits, target):
    peak = jnp.max(logits, axis=0, keepdims=True)
    expo = jnp.exp(logits - peak)
    total = jnp.sum(expo, axis=0, keepdims=True)
    mean = jnp.sum(expo * logits, axis=0, keepdims=True) / total
    cross = jnp.sum(target * logits, axis=0, keepdims=True)
    lse = peak + jnp.log(total)
    row = lax.broadcasted_iota(jnp.int32, (8, LANES), 0)
    return jnp.where(row == 0, lse, jnp.where(row == 1, mean, jnp.where(row == 2, cross, 0.0)))


def first_kernel(pos, got, source, own, own2, next1, next2, w, out, target, held, teach, sems):
    core = pos[1]
    half = source.shape[0] // 2
    pieces = (slice(0, half), slice(half, 2 * half))
    copies = [
        pltpu.make_async_copy(
            source.at[pl.ds(at.start, at.stop - at.start)], w.at[pl.ds(at.start, at.stop - at.start)], sems.at[k]
        )
        for k, at in enumerate(pieces)
    ]
    copies[0].start()
    mine, other = core * 64, (1 - core) * 64
    for block, row in ((own, mine), (own2, other), (next1, 128 + mine), (next2, 128 + other)):
        held[pl.ds(pl.multiple_of(row, 64), 64)] = block[...]
    flipped = got[...].T
    source_row = lax.broadcasted_iota(jnp.int32, (LANES, 4 * LANES), 0)
    token = lax.broadcasted_iota(jnp.int32, (LANES, 4 * LANES), 1)
    spread = jnp.zeros((16, 4 * LANES), jnp.float32)
    for row in range(4):
        pick = (token == source_row * 4 + row).astype(jnp.float32)
        spread = spread + jnp.dot(
            flipped[row * 16 : row * 16 + 16], pick,
            precision=lax.Precision.HIGHEST, preferred_element_type=jnp.float32,
        )
    for block in range(4):
        teach[block] = spread[:, block * LANES : (block + 1) * LANES]
    rows = 32
    low_iota = lax.broadcasted_iota(jnp.int32, (rows, LANES), 0).astype(jnp.float32)
    for slot in range(4):
        info = teach[plane(pos, slot)]
        groups, values = [], []
        for k in range(SLOTS):
            index = info[8 + k : 9 + k]
            group = jnp.floor(index * (1.0 / rows))
            groups.append(group)
            values.append(jnp.where(low_iota == index - group * rows, info[k : k + 1], 0.0))

        @pl.loop(0, w.shape[0] // rows, unroll=4)
        def _(step):
            number = jnp.full((1, LANES), step, jnp.int32).astype(jnp.float32)
            dense = jnp.zeros((rows, LANES), jnp.float32)
            for group, value in zip(groups, values):
                dense = dense + jnp.where(group == number, value, 0.0)
            target[slot, pl.ds(pl.multiple_of(step * rows, rows), rows)] = dense

    for k, at in enumerate(pieces):
        copies[k].wait()
        if k + 1 < len(pieces):
            copies[k + 1].start()
        logits = dot_nt(held[...], w[at]).T
        for slot in range(2):
            out[slot, at] = logits[:, slot * LANES : (slot + 1) * LANES]


def first_logits(pos, got, source, blocks):
    vocab, width = source.shape
    return pl.pallas_call(
        first_kernel,
        in_specs=[SCALARS, WHOLE, FAR] + [WHOLE] * 4,
        out_specs=[WHOLE] * 4,
        out_shape=[
            pltpu.VMEM((vocab, width), jnp.bfloat16),
            jax.ShapeDtypeStruct((2, vocab, LANES), jnp.float32),
            jax.ShapeDtypeStruct((4, vocab, LANES), jnp.float32),
            jax.ShapeDtypeStruct((2 * LANES, width), jnp.bfloat16),
        ],
        scratch_shapes=[pltpu.VMEM((4, 16, LANES), jnp.float32), pltpu.SemaphoreType.DMA((2,))],
        compiler_params=params(),
        cost_estimate=cost(1e11, 1e9),
    )(pos, got, pltpu.with_memory_space_constraint(source, pltpu.HBM), *blocks)


def spread_stats(info):
    lane = lax.broadcasted_iota(jnp.int32, (32, LANES), 1)
    row = lax.broadcasted_iota(jnp.int32, (32, LANES), 0)
    extra = jnp.zeros((32, LANES), jnp.float32)
    for kind in range(3):
        for token in range(4):
            value = jnp.sum(jnp.where(lane == row * 4 + token, info[kind : kind + 1], 0.0), axis=1, keepdims=True)
            extra = extra + jnp.where(lane == kind * 4 + token, value, 0.0)
    return extra


def fill_send(send, block, info):
    send[:, pl.ds(pl.multiple_of(block * LANES, LANES), LANES)] = jnp.broadcast_to(info[0:1], (LANES, LANES))
    send[pl.ds(pl.multiple_of(block * 32, 32), 32), 4 * LANES : 5 * LANES] = spread_stats(info)


def stats_kernel(pos, logits, target, send):
    for slot in range(2):
        fill_send(send, plane(pos, slot), local_stats(logits[slot], target[slot]))


def near_stats(pos, logits, target):
    return pl.pallas_call(
        stats_kernel,
        in_specs=[SCALARS] + [WHOLE] * 2,
        out_specs=WHOLE,
        out_shape=jax.ShapeDtypeStruct((LANES, 5 * LANES), jnp.float32),
        compiler_params=params(),
        cost_estimate=cost(1000, 1000),
    )(pos, logits, target)


def last_kernel(pos, w, target, early, back1, back2, far, far2, out, send, held):
    core = pos[1]
    mine, other = core * 64, (1 - core) * 64
    for block, row in ((back1, other), (back2, mine), (far, 128 + mine), (far2, 128 + other)):
        held[pl.ds(pl.multiple_of(row, 64), 64)] = block[...]
    logits = dot_nt(w[...], held[...])
    for block in range(5):
        at = slice(block * LANES, (block + 1) * LANES)
        send[:, at] = early[:, at]
    for slot in range(2):
        out[slot] = logits[:, slot * LANES : (slot + 1) * LANES]
    for slot in range(2):
        fill_send(send, plane(pos, 2 + slot), local_stats(out[slot], target[2 + slot]))


def last_logits(pos, w, target, early, blocks):
    vocab, width = w.shape
    return pl.pallas_call(
        last_kernel,
        in_specs=[SCALARS] + [WHOLE] * 7,
        out_specs=[WHOLE] * 3,
        out_shape=[
            jax.ShapeDtypeStruct((2, vocab, LANES), jnp.float32),
            jax.ShapeDtypeStruct((LANES, 5 * LANES), jnp.float32),
            jax.ShapeDtypeStruct((2 * LANES, width), jnp.bfloat16),
        ],
        compiler_params=params(),
        cost_estimate=cost(2 * vocab * width * 256, vocab * width * 2),
    )(pos, w, target, early, *blocks)


def grad_of(logits, lse, target):
    return loss_scale * (jnp.exp(logits - lse) - target)


def split_dot(left, w, mine_out, other_out):
    for tile in range(w.shape[1] // COLS):
        at = slice(tile * COLS, (tile + 1) * COLS)
        grad = jnp.dot(left[...], w[:, at], preferred_element_type=jnp.float32)
        for slot in range(left.shape[0] // LANES):
            to, base = slice(slot * 64, (slot + 1) * 64), slot * LANES
            mine_out[to, at] = grad[base : base + 64]
            other_out[to, at] = grad[base + 64 : base + LANES].astype(jnp.bfloat16)


def far_grad_kernel(pos, stats, logits, target, w, mine_out, other_out, grad_out, lse_out, loss_out, flipped, left):
    parts = stats[:, : 4 * LANES]
    peak = jnp.max(parts, axis=0, keepdims=True)
    lse = peak + jnp.log(jnp.sum(jnp.exp(parts - peak), axis=0, keepdims=True))
    for block in range(4):
        lse_out[block] = jnp.broadcast_to(lse[:, block * LANES : (block + 1) * LANES], (8, LANES))
    few = stats[:, 4 * LANES :]
    peak = jnp.max(few, axis=0, keepdims=True)
    weight = jnp.exp(few - peak)
    total = jnp.sum(weight, axis=0, keepdims=True)
    mean = jnp.sum(weight * pltpu.roll(few, LANES - 4, 1), axis=0, keepdims=True) / total
    cross = jnp.sum(pltpu.roll(few, LANES - 8, 1), axis=0, keepdims=True)
    lse4 = peak + jnp.log(total)
    row = lax.broadcasted_iota(jnp.int32, (8, LANES), 0)
    loss_out[...] = jnp.where(row == 0, lse4 - cross, lse4 - mean)
    far = lse_out[plane(pos, 3)]
    grad = grad_of(logits[1], far[0:1], target[3])
    grad_out[...] = grad.astype(jnp.bfloat16)
    core = pos[1]
    flipped[...] = grad.T.astype(jnp.bfloat16)
    left[:64, :] = flipped[pl.ds(pl.multiple_of(core * 64, 64), 64)]
    left[64:, :] = flipped[pl.ds(pl.multiple_of((1 - core) * 64, 64), 64)]
    split_dot(left, w, mine_out, other_out)


def far_grad(pos, stats, logits, target, w):
    vocab, width = w.shape
    return pl.pallas_call(
        far_grad_kernel,
        in_specs=[SCALARS] + [WHOLE] * 4,
        out_specs=[WHOLE] * 5,
        out_shape=[
            jax.ShapeDtypeStruct((64, width), jnp.float32),
            jax.ShapeDtypeStruct((64, width), jnp.bfloat16),
            jax.ShapeDtypeStruct((vocab, LANES), jnp.bfloat16),
            jax.ShapeDtypeStruct((4, 8, LANES), jnp.float32),
            jax.ShapeDtypeStruct((8, LANES), jnp.float32),
        ],
        scratch_shapes=[pltpu.VMEM((LANES, vocab), jnp.bfloat16)] * 2,
        compiler_params=params(),
        cost_estimate=cost(2 * vocab * width * 128, vocab * width * 2),
    )(pos, stats, logits, target, w)


def grads_kernel(pos, logits, last, target, lse, far, wide_out, first_out, second_out, flipped):
    core = pos[1]
    mine, other = pl.ds(pl.multiple_of(core * 64, 64), 64), pl.ds(pl.multiple_of((1 - core) * 64, 64), 64)
    for slot in (2, 1, 0):
        part = last[0] if slot == 2 else logits[slot]
        grad = grad_of(part, lse[plane(pos, slot)][0:1], target[slot])
        wide_out[:, slot * LANES : (slot + 1) * LANES] = grad.astype(jnp.bfloat16)
        flipped[...] = grad.T.astype(jnp.bfloat16)
        if slot == 2:
            first_out[:64, :] = flipped[other]
            second_out[:64, :] = flipped[mine]
        elif slot == 1:
            first_out[64:, :] = flipped[mine]
            second_out[64:128, :] = flipped[other]
        else:
            second_out[128:192, :] = flipped[mine]
            second_out[192:, :] = flipped[other]
    wide_out[:, 3 * LANES :] = far[...]


def near_grads(pos, logits, last, target, lse, far):
    vocab = far.shape[0]
    return pl.pallas_call(
        grads_kernel,
        in_specs=[SCALARS] + [WHOLE] * 5,
        out_specs=[WHOLE] * 3,
        out_shape=[
            jax.ShapeDtypeStruct((vocab, 4 * LANES), jnp.bfloat16),
            jax.ShapeDtypeStruct((LANES, vocab), jnp.bfloat16),
            jax.ShapeDtypeStruct((2 * LANES, vocab), jnp.bfloat16),
        ],
        scratch_shapes=[pltpu.VMEM((LANES, vocab), jnp.bfloat16)],
        compiler_params=params(),
        cost_estimate=cost(2e6, 5e6),
    )(pos, logits, last, target, lse, far)


def near_kernel(left, w, mine_out, other_out):
    split_dot(left, w, mine_out, other_out)


def near_grad(left, w):
    vocab, width = w.shape
    tokens = left.shape[0]
    return pl.pallas_call(
        near_kernel,
        in_specs=[WHOLE] * 2,
        out_specs=[WHOLE] * 2,
        out_shape=[
            jax.ShapeDtypeStruct((tokens // 2, width), jnp.float32),
            jax.ShapeDtypeStruct((tokens // 2, width), jnp.bfloat16),
        ],
        compiler_params=params(),
        cost_estimate=cost(2 * vocab * width * tokens, vocab * width * 2),
    )(left, w)


def weight_kernel(grad, near, far, out):
    for tile in range(out.shape[1] // COLS):
        at = slice(tile * COLS, (tile + 1) * COLS)
        held = jnp.concatenate([near[:, at], far[:, at]], axis=0)
        out[:, at] = jnp.dot(grad[...], held, preferred_element_type=jnp.float32).astype(jnp.bfloat16)


def weight_grad(grad, near, far):
    vocab, tokens = grad.shape
    width = near.shape[1]
    rows = 256
    return pl.pallas_call(
        weight_kernel,
        grid=(vocab // rows,),
        in_specs=[pl.BlockSpec((rows, tokens), lambda i: (i, 0)), WHOLE, WHOLE],
        out_specs=pl.BlockSpec((rows, width), lambda i: (i, 0)),
        out_shape=jax.ShapeDtypeStruct((vocab, width), jnp.bfloat16),
        compiler_params=params(),
        cost_estimate=cost(2 * vocab * width * tokens, vocab * width * 2 + tokens * width * 2),
    )(grad, near, far)


def widen_kernel(block, out):
    out[...] = block[...].astype(jnp.float32)


def widen(block):
    return pl.pallas_call(
        widen_kernel,
        in_specs=[WHOLE],
        out_specs=WHOLE,
        out_shape=jax.ShapeDtypeStruct(block.shape, jnp.float32),
        compiler_params=params(),
        cost_estimate=cost(1e11, 1e9),
    )(block)


def gather_own_kernel(mine, swap, across, out):
    rows = out.shape[0]
    f32 = jnp.float32
    out[...] = mine[rows:] + swap[rows:].astype(f32) + across[...].astype(f32)


def gather_own(mine, swap, across):
    return pl.pallas_call(
        gather_own_kernel,
        in_specs=[WHOLE] * 3,
        out_specs=WHOLE,
        out_shape=jax.ShapeDtypeStruct(across.shape, jnp.float32),
        compiler_params=params(),
        cost_estimate=cost(1e11, 1e9),
    )(mine, swap, across)


def fold_kernel(near, arrived, out, total):
    total[...] = (near[...] + arrived[...].astype(jnp.float32)).astype(jnp.bfloat16)
    part = out.shape[2]
    for index in range(out.shape[0]):
        out[index] = total[:, index * part : (index + 1) * part]


def fold(count, near, arrived):
    rows, width = near.shape
    return pl.pallas_call(
        fold_kernel,
        in_specs=[WHOLE] * 2,
        out_specs=WHOLE,
        out_shape=jax.ShapeDtypeStruct((count, rows, width // count), jnp.bfloat16),
        scratch_shapes=[pltpu.VMEM((rows, width), jnp.bfloat16)],
        compiler_params=params(),
        cost_estimate=cost(2e6, 4e6),
    )(near, arrived)


def sum_kernel(parts, out):
    total = parts[0].astype(jnp.float32)
    for index in range(1, parts.shape[0]):
        total = total + parts[index].astype(jnp.float32)
    out[...] = total.astype(jnp.bfloat16)


def sum_parts(parts):
    return pl.pallas_call(
        sum_kernel,
        in_specs=[WHOLE],
        out_specs=WHOLE,
        out_shape=jax.ShapeDtypeStruct(parts.shape[1:], jnp.bfloat16),
        compiler_params=params(),
        cost_estimate=cost(4e5, 8e5),
    )(parts)


def body(hidden, head_weight, teacher_logits, teacher_ids):
    seq_count = lax.axis_size("seq")
    vocab_count = lax.axis_size("vocab")
    owners = seq_count * vocab_count
    vocab_rows, width = head_weight.shape
    tok_rows, feat_part = hidden.shape
    seq_index = lax.axis_index("seq")
    pos = jnp.stack([seq_index // 2, seq_index % 2]).astype(jnp.int32)
    ring = [(i, (i + 2 - 4 * (i % 2)) % seq_count) for i in range(seq_count)]
    cross = [(i, (i + 2 - 4 * (i % 2)) % seq_count ^ 1) for i in range(seq_count)]
    twin = [(i, i ^ 1) for i in range(seq_count)]

    def move(x, perm):
        return lax.ppermute(x, "seq", perm)

    def after(x, *before):
        return lax.optimization_barrier((x, before))[0]

    f32 = jnp.float32
    bf16 = jnp.bfloat16

    hidden, pos = lax.optimization_barrier((hidden, pos))
    spread = copies_of(hidden, vocab_count)
    spread = lax.all_to_all(spread, "vocab", split_axis=0, concat_axis=0, tiled=True)
    own = join_parts(spread)
    next1 = move(own, ring)
    own2 = move(own, twin)
    next2 = move(own2, ring)
    teacher_logits, own2 = lax.optimization_barrier((teacher_logits, own2))
    teach = teacher_rows(owners, vocab_rows, teacher_logits, teacher_ids)
    got = lax.all_to_all(teach, BOTH, split_axis=0, concat_axis=0, tiled=True)
    far = move(next1, ring)
    near_blocks = (own, own2, next1, next2)
    weight, logits, target, near_rows = first_logits(pos, got, head_weight, near_blocks)
    back = (move(next1, twin), move(after(next2, got), twin))
    far = after(far, logits)
    early = near_stats(pos, after(logits, back[1]), target)
    last, send, last_rows = last_logits(pos, weight, target, early, (*back, far, move(far, twin)))
    stats = lax.all_to_all(send, BOTH, split_axis=0, concat_axis=0, tiled=True)

    far_mine, far_other, grad_far, lse, loss = far_grad(pos, stats, last, target, weight)
    far_swap = move(far_other, twin)
    wide, first_left, second_left = near_grads(pos, logits, last, target, lse, grad_far)
    first_mine, first_other = near_grad(first_left, weight)
    first_swap = move(first_other, twin)
    far_sum = (far_mine + far_swap.astype(f32)).astype(bf16)
    passed = move(far_sum, ring)
    second_left = after(second_left, far_sum, first_other)
    second_mine, second_other = near_grad(second_left, weight)
    second_swap = move(second_other, twin)
    first_sum = (first_mine + first_swap.astype(f32)).astype(bf16)
    first = move(first_sum, cross)
    passed = widen(after(passed, first_sum))
    second_sum = second_mine[:tok_rows] + second_swap[:tok_rows].astype(f32)
    second_sum = (second_sum + passed).astype(bf16)
    second = move(second_sum, ring)
    rows = teacher_logits.shape[0]
    loss = after(loss, second_sum)
    cross_entropy, entropy = loss[0, :rows], loss[1, :rows]
    wide = after(wide, second_sum, cross_entropy, entropy)
    grad_weight = weight_grad(wide, near_rows, last_rows)
    first = after(first, grad_weight)
    gathered = gather_own(second_mine, second_swap, first)
    second, gathered = lax.optimization_barrier((second, gathered))
    parts = fold(vocab_count, gathered, second)
    parts = lax.all_to_all(parts, "vocab", split_axis=0, concat_axis=0, tiled=True)
    grad_hidden = sum_parts(parts)
    return cross_entropy, entropy, grad_hidden, grad_weight


def solution(mesh):
    placed = (
        P("seq", "vocab"),
        P(("seq", "vocab"), None),
        P(("seq", "vocab"), None),
        P(("seq", "vocab"), None),
    )
    return jax.shard_map(
        body,
        mesh=mesh,
        in_specs=placed,
        out_specs=(
            P(("seq", "vocab")),
            P(("seq", "vocab")),
            P("seq", "vocab"),
            P(("seq", "vocab"), None),
        ),
        check_vma=False,
    )
```

```python
import functools

import jax
import jax.numpy as jnp
from jax import lax
from jax.experimental import pallas as pl
from jax.experimental.pallas import tpu as pltpu
from jax.sharding import PartitionSpec as P

loss_scale = 64.0
SLOTS = 6
LANES = 128
COLS = 768
ANY = pl.BlockSpec(memory_space=pl.ANY)
WHOLE = pl.BlockSpec(memory_space=pltpu.VMEM)
FAR = pl.BlockSpec(memory_space=pltpu.HBM)
SCALARS = pl.BlockSpec(memory_space=pltpu.SMEM)
VMEM_LIMIT = 16 * 1024 * 1024
BOTH = ("seq", "vocab")


def plane(pos, slot):
    z, core = pos[0], pos[1]
    return (z + (0, 3 - 2 * core, 1 + 2 * core, 2)[slot]) % 4


def params():
    return pltpu.CompilerParams(vmem_limit_bytes=VMEM_LIMIT)


def cost(flops, nbytes):
    return pl.CostEstimate(flops=int(flops), bytes_accessed=int(nbytes), transcendentals=0)


def teacher_kernel(owners, vocab_rows, logits_ref, ids_ref, out_ref):
    rows, width = logits_ref.shape
    scores = logits_ref[...]
    expo = jnp.exp(scores - jnp.max(scores, axis=1, keepdims=True))
    prob = expo / jnp.sum(expo, axis=1, keepdims=True)
    ids = ids_ref[...]
    shift = vocab_rows.bit_length() - 1
    owner_of = lax.shift_right_logical(ids, shift)
    local_of = (ids - owner_of * vocab_rows + 1).astype(jnp.float32)
    owner_of = owner_of.astype(jnp.float32)
    owner_iota = lax.broadcasted_iota(jnp.int32, (owners, width), 0).astype(jnp.float32)
    slot_iota = lax.broadcasted_iota(jnp.int32, (owners, width), 1).astype(jnp.float32)
    lane = lax.broadcasted_iota(jnp.int32, (owners, rows * 16), 1)
    out = jnp.zeros((owners, rows * 16), jnp.float32)
    for row in range(rows):
        row_prob = jnp.broadcast_to(prob[row : row + 1, :], (owners, width))
        owner = jnp.broadcast_to(owner_of[row : row + 1, :], (owners, width))
        local = jnp.broadcast_to(local_of[row : row + 1, :], (owners, width))
        same = owner == owner_iota
        start = jnp.sum(jnp.where(owner < owner_iota, 1.0, 0.0), axis=1, keepdims=True)
        place = jnp.where(same, slot_iota - start, -1.0)
        for slot in range(2):
            hit = place == slot
            value = jnp.sum(jnp.where(hit, row_prob, 0.0), axis=1, keepdims=True)
            index = jnp.sum(jnp.where(hit, local, 0.0), axis=1, keepdims=True) - 1.0
            out = out + jnp.where(lane == row * 16 + slot, value, jnp.where(lane == row * 16 + 8 + slot, index, 0.0))
        many = jnp.sum(jnp.where(same, 1.0, 0.0), axis=1, keepdims=True) > 2.0
        first = jnp.sum(jnp.where(many, start, 0.0), axis=0, keepdims=True)
        hot_place = slot_iota[:1] - first
        hot_index = local_of[row : row + 1, :]
        extra = jnp.zeros((1, rows * 16), jnp.float32)
        for slot in range(2, SLOTS):
            hit = hot_place == slot
            value = jnp.sum(jnp.where(hit, prob[row : row + 1, :], 0.0), axis=1, keepdims=True)
            index = jnp.sum(jnp.where(hit, hot_index, 0.0), axis=1, keepdims=True)
            at = lane[:1]
            extra = extra + jnp.where(at == row * 16 + slot, value, jnp.where(at == row * 16 + 8 + slot, index, 0.0))
        empty = (lane >= row * 16 + 10) & (lane < row * 16 + 8 + SLOTS)
        out = out + jnp.where(many, extra, 0.0) - empty.astype(jnp.float32)
    out_ref[...] = out


def teacher_rows(owners, vocab_rows, teacher_logits, teacher_ids):
    rows = teacher_logits.shape[0]
    return pl.pallas_call(
        functools.partial(teacher_kernel, owners, vocab_rows),
        out_shape=jax.ShapeDtypeStruct((owners, rows * 16), jnp.float32),
        compiler_params=params(),
        cost_estimate=cost(4e6, 40000),
    )(teacher_logits, teacher_ids)


def copies_kernel(block, out):
    for index in range(out.shape[0]):
        out[index] = block[...]


def copies_of(block, count):
    return pl.pallas_call(
        copies_kernel,
        in_specs=[WHOLE],
        out_specs=WHOLE,
        out_shape=jax.ShapeDtypeStruct((count, *block.shape), block.dtype),
        compiler_params=params(),
        cost_estimate=cost(1000, 1e6),
    )(block)


def join_kernel(parts, out, rows):
    part = parts.shape[2]
    for index in range(parts.shape[0]):
        rows[:, index * part : (index + 1) * part] = parts[index].astype(jnp.float32)
    out[...] = rows[...].astype(jnp.bfloat16)


def join_parts(parts):
    count, rows, part = parts.shape
    return pl.pallas_call(
        join_kernel,
        in_specs=[WHOLE],
        out_specs=WHOLE,
        out_shape=jax.ShapeDtypeStruct((rows, count * part), parts.dtype),
        scratch_shapes=[pltpu.VMEM((rows, count * part), jnp.float32)],
        compiler_params=params(),
        cost_estimate=cost(1e6, 2e6),
    )(parts)


def dot_nt(a, b):
    return lax.dot_general(a, b, (((1,), (1,)), ((), ())), preferred_element_type=jnp.float32)


def local_stats(logits, target):
    peak = jnp.max(logits, axis=0, keepdims=True)
    expo = jnp.exp(logits - peak)
    total = jnp.sum(expo, axis=0, keepdims=True)
    mean = jnp.sum(expo * logits, axis=0, keepdims=True) / total
    cross = jnp.sum(target * logits, axis=0, keepdims=True)
    lse = peak + jnp.log(total)
    row = lax.broadcasted_iota(jnp.int32, (8, LANES), 0)
    return jnp.where(row == 0, lse, jnp.where(row == 1, mean, jnp.where(row == 2, cross, 0.0)))


def first_kernel(pos, got, source, own, own2, next1, next2, w, out, target, held, teach, sems):
    core = pos[1]
    half = source.shape[0] // 2
    pieces = (slice(0, half), slice(half, 2 * half))
    copies = [
        pltpu.make_async_copy(
            source.at[pl.ds(at.start, at.stop - at.start)], w.at[pl.ds(at.start, at.stop - at.start)], sems.at[k]
        )
        for k, at in enumerate(pieces)
    ]
    copies[0].start()
    mine, other = core * 64, (1 - core) * 64
    for block, row in ((own, mine), (own2, other), (next1, 128 + mine), (next2, 128 + other)):
        held[pl.ds(pl.multiple_of(row, 64), 64)] = block[...]
    flipped = got[...].T
    source_row = lax.broadcasted_iota(jnp.int32, (LANES, 4 * LANES), 0)
    token = lax.broadcasted_iota(jnp.int32, (LANES, 4 * LANES), 1)
    spread = jnp.zeros((16, 4 * LANES), jnp.float32)
    for row in range(4):
        pick = (token == source_row * 4 + row).astype(jnp.float32)
        spread = spread + jnp.dot(
            flipped[row * 16 : row * 16 + 16], pick,
            precision=lax.Precision.HIGHEST, preferred_element_type=jnp.float32,
        )
    for block in range(4):
        teach[block] = spread[:, block * LANES : (block + 1) * LANES]
    rows = 32
    low_iota = lax.broadcasted_iota(jnp.int32, (rows, LANES), 0).astype(jnp.float32)
    for slot in range(4):
        info = teach[plane(pos, slot)]
        groups, values = [], []
        for k in range(SLOTS):
            index = info[8 + k : 9 + k]
            group = jnp.floor(index * (1.0 / rows))
            groups.append(group)
            values.append(jnp.where(low_iota == index - group * rows, info[k : k + 1], 0.0))

        @pl.loop(0, w.shape[0] // rows, unroll=4)
        def _(step):
            number = jnp.full((1, LANES), step, jnp.int32).astype(jnp.float32)
            dense = jnp.zeros((rows, LANES), jnp.float32)
            for group, value in zip(groups, values):
                dense = dense + jnp.where(group == number, value, 0.0)
            target[slot, pl.ds(pl.multiple_of(step * rows, rows), rows)] = dense

    for k, at in enumerate(pieces):
        copies[k].wait()
        if k + 1 < len(pieces):
            copies[k + 1].start()
        logits = dot_nt(held[...], w[at]).T
        for slot in range(2):
            out[slot, at] = logits[:, slot * LANES : (slot + 1) * LANES]


def first_logits(pos, got, source, blocks):
    vocab, width = source.shape
    return pl.pallas_call(
        first_kernel,
        in_specs=[SCALARS, WHOLE, FAR] + [WHOLE] * 4,
        out_specs=[WHOLE] * 4,
        out_shape=[
            pltpu.VMEM((vocab, width), jnp.bfloat16),
            jax.ShapeDtypeStruct((2, vocab, LANES), jnp.float32),
            jax.ShapeDtypeStruct((4, vocab, LANES), jnp.float32),
            jax.ShapeDtypeStruct((2 * LANES, width), jnp.bfloat16),
        ],
        scratch_shapes=[pltpu.VMEM((4, 16, LANES), jnp.float32), pltpu.SemaphoreType.DMA((2,))],
        compiler_params=params(),
        cost_estimate=cost(1e11, 1e9),
    )(pos, got, pltpu.with_memory_space_constraint(source, pltpu.HBM), *blocks)


def spread_stats(info):
    lane = lax.broadcasted_iota(jnp.int32, (32, LANES), 1)
    row = lax.broadcasted_iota(jnp.int32, (32, LANES), 0)
    extra = jnp.zeros((32, LANES), jnp.float32)
    for kind in range(3):
        for token in range(4):
            value = jnp.sum(jnp.where(lane == row * 4 + token, info[kind : kind + 1], 0.0), axis=1, keepdims=True)
            extra = extra + jnp.where(lane == kind * 4 + token, value, 0.0)
    return extra


def fill_send(send, block, info):
    send[:, pl.ds(pl.multiple_of(block * LANES, LANES), LANES)] = jnp.broadcast_to(info[0:1], (LANES, LANES))
    send[pl.ds(pl.multiple_of(block * 32, 32), 32), 4 * LANES : 5 * LANES] = spread_stats(info)


def stats_kernel(pos, logits, target, send):
    for slot in range(2):
        fill_send(send, plane(pos, slot), local_stats(logits[slot], target[slot]))


def near_stats(pos, logits, target):
    return pl.pallas_call(
        stats_kernel,
        in_specs=[SCALARS] + [WHOLE] * 2,
        out_specs=WHOLE,
        out_shape=jax.ShapeDtypeStruct((LANES, 5 * LANES), jnp.float32),
        compiler_params=params(),
        cost_estimate=cost(1000, 1000),
    )(pos, logits, target)


def last_kernel(pos, w, target, early, back1, back2, far, far2, out, send, held):
    core = pos[1]
    mine, other = core * 64, (1 - core) * 64
    for block, row in ((back1, other), (back2, mine), (far, 128 + mine), (far2, 128 + other)):
        held[pl.ds(pl.multiple_of(row, 64), 64)] = block[...]
    logits = dot_nt(w[...], held[...])
    for block in range(5):
        at = slice(block * LANES, (block + 1) * LANES)
        send[:, at] = early[:, at]
    for slot in range(2):
        out[slot] = logits[:, slot * LANES : (slot + 1) * LANES]
    for slot in range(2):
        fill_send(send, plane(pos, 2 + slot), local_stats(out[slot], target[2 + slot]))


def last_logits(pos, w, target, early, blocks):
    vocab, width = w.shape
    return pl.pallas_call(
        last_kernel,
        in_specs=[SCALARS] + [WHOLE] * 7,
        out_specs=[WHOLE] * 3,
        out_shape=[
            jax.ShapeDtypeStruct((2, vocab, LANES), jnp.float32),
            jax.ShapeDtypeStruct((LANES, 5 * LANES), jnp.float32),
            jax.ShapeDtypeStruct((2 * LANES, width), jnp.bfloat16),
        ],
        compiler_params=params(),
        cost_estimate=cost(2 * vocab * width * 256, vocab * width * 2),
    )(pos, w, target, early, *blocks)


def grad_of(logits, lse, target):
    return loss_scale * (jnp.exp(logits - lse) - target)


def split_dot(left, w, mine_out, other_out):
    for tile in range(w.shape[1] // COLS):
        at = slice(tile * COLS, (tile + 1) * COLS)
        grad = jnp.dot(left[...], w[:, at], preferred_element_type=jnp.float32)
        for slot in range(left.shape[0] // LANES):
            to, base = slice(slot * 64, (slot + 1) * 64), slot * LANES
            mine_out[to, at] = grad[base : base + 64]
            other_out[to, at] = grad[base + 64 : base + LANES].astype(jnp.bfloat16)


def far_grad_kernel(pos, stats, logits, target, w, mine_out, other_out, grad_out, lse_out, loss_out, flipped, left):
    parts = stats[:, : 4 * LANES]
    peak = jnp.max(parts, axis=0, keepdims=True)
    lse = peak + jnp.log(jnp.sum(jnp.exp(parts - peak), axis=0, keepdims=True))
    for block in range(4):
        lse_out[block] = jnp.broadcast_to(lse[:, block * LANES : (block + 1) * LANES], (8, LANES))
    few = stats[:, 4 * LANES :]
    peak = jnp.max(few, axis=0, keepdims=True)
    weight = jnp.exp(few - peak)
    total = jnp.sum(weight, axis=0, keepdims=True)
    mean = jnp.sum(weight * pltpu.roll(few, LANES - 4, 1), axis=0, keepdims=True) / total
    cross = jnp.sum(pltpu.roll(few, LANES - 8, 1), axis=0, keepdims=True)
    lse4 = peak + jnp.log(total)
    row = lax.broadcasted_iota(jnp.int32, (8, LANES), 0)
    loss_out[...] = jnp.where(row == 0, lse4 - cross, lse4 - mean)
    far = lse_out[plane(pos, 3)]
    grad = grad_of(logits[1], far[0:1], target[3])
    grad_out[...] = grad.astype(jnp.bfloat16)
    core = pos[1]
    flipped[...] = grad.T.astype(jnp.bfloat16)
    left[:64, :] = flipped[pl.ds(pl.multiple_of(core * 64, 64), 64)]
    left[64:, :] = flipped[pl.ds(pl.multiple_of((1 - core) * 64, 64), 64)]
    split_dot(left, w, mine_out, other_out)


def far_grad(pos, stats, logits, target, w):
    vocab, width = w.shape
    return pl.pallas_call(
        far_grad_kernel,
        in_specs=[SCALARS] + [WHOLE] * 4,
        out_specs=[WHOLE] * 5,
        out_shape=[
            jax.ShapeDtypeStruct((64, width), jnp.float32),
            jax.ShapeDtypeStruct((64, width), jnp.bfloat16),
            jax.ShapeDtypeStruct((vocab, LANES), jnp.bfloat16),
            jax.ShapeDtypeStruct((4, 8, LANES), jnp.float32),
            jax.ShapeDtypeStruct((8, LANES), jnp.float32),
        ],
        scratch_shapes=[pltpu.VMEM((LANES, vocab), jnp.bfloat16)] * 2,
        compiler_params=params(),
        cost_estimate=cost(2 * vocab * width * 128, vocab * width * 2),
    )(pos, stats, logits, target, w)


def grads_kernel(pos, logits, last, target, lse, far, wide_out, first_out, second_out, flipped):
    core = pos[1]
    mine, other = pl.ds(pl.multiple_of(core * 64, 64), 64), pl.ds(pl.multiple_of((1 - core) * 64, 64), 64)
    for slot in (2, 1, 0):
        part = last[0] if slot == 2 else logits[slot]
        grad = grad_of(part, lse[plane(pos, slot)][0:1], target[slot])
        wide_out[:, slot * LANES : (slot + 1) * LANES] = grad.astype(jnp.bfloat16)
        flipped[...] = grad.T.astype(jnp.bfloat16)
        if slot == 2:
            first_out[:64, :] = flipped[other]
            second_out[:64, :] = flipped[mine]
        elif slot == 1:
            first_out[64:, :] = flipped[mine]
            second_out[64:128, :] = flipped[other]
        else:
            second_out[128:192, :] = flipped[mine]
            second_out[192:, :] = flipped[other]
    wide_out[:, 3 * LANES :] = far[...]


def near_grads(pos, logits, last, target, lse, far):
    vocab = far.shape[0]
    return pl.pallas_call(
        grads_kernel,
        in_specs=[SCALARS] + [WHOLE] * 5,
        out_specs=[WHOLE] * 3,
        out_shape=[
            jax.ShapeDtypeStruct((vocab, 4 * LANES), jnp.bfloat16),
            jax.ShapeDtypeStruct((LANES, vocab), jnp.bfloat16),
            jax.ShapeDtypeStruct((2 * LANES, vocab), jnp.bfloat16),
        ],
        scratch_shapes=[pltpu.VMEM((LANES, vocab), jnp.bfloat16)],
        compiler_params=params(),
        cost_estimate=cost(2e6, 5e6),
    )(pos, logits, last, target, lse, far)


def near_kernel(left, w, mine_out, other_out):
    split_dot(left, w, mine_out, other_out)


def near_grad(left, w):
    vocab, width = w.shape
    tokens = left.shape[0]
    return pl.pallas_call(
        near_kernel,
        in_specs=[WHOLE] * 2,
        out_specs=[WHOLE] * 2,
        out_shape=[
            jax.ShapeDtypeStruct((tokens // 2, width), jnp.float32),
            jax.ShapeDtypeStruct((tokens // 2, width), jnp.bfloat16),
        ],
        compiler_params=params(),
        cost_estimate=cost(2 * vocab * width * tokens, vocab * width * 2),
    )(left, w)


def weight_kernel(grad, near, far, out):
    for tile in range(out.shape[1] // COLS):
        at = slice(tile * COLS, (tile + 1) * COLS)
        held = jnp.concatenate([near[:, at], far[:, at]], axis=0)
        out[:, at] = jnp.dot(grad[...], held, preferred_element_type=jnp.float32).astype(jnp.bfloat16)


def weight_grad(grad, near, far):
    vocab, tokens = grad.shape
    width = near.shape[1]
    rows = 256
    return pl.pallas_call(
        weight_kernel,
        grid=(vocab // rows,),
        in_specs=[pl.BlockSpec((rows, tokens), lambda i: (i, 0)), WHOLE, WHOLE],
        out_specs=pl.BlockSpec((rows, width), lambda i: (i, 0)),
        out_shape=jax.ShapeDtypeStruct((vocab, width), jnp.bfloat16),
        compiler_params=params(),
        cost_estimate=cost(2 * vocab * width * tokens, vocab * width * 2 + tokens * width * 2),
    )(grad, near, far)


def widen_kernel(block, out):
    out[...] = block[...].astype(jnp.float32)


def widen(block):
    return pl.pallas_call(
        widen_kernel,
        in_specs=[WHOLE],
        out_specs=WHOLE,
        out_shape=jax.ShapeDtypeStruct(block.shape, jnp.float32),
        compiler_params=params(),
        cost_estimate=cost(1e11, 1e9),
    )(block)


def gather_own_kernel(mine, swap, across, out):
    rows = out.shape[0]
    f32 = jnp.float32
    out[...] = mine[rows:] + swap[rows:].astype(f32) + across[...].astype(f32)


def gather_own(mine, swap, across):
    return pl.pallas_call(
        gather_own_kernel,
        in_specs=[WHOLE] * 3,
        out_specs=WHOLE,
        out_shape=jax.ShapeDtypeStruct(across.shape, jnp.float32),
        compiler_params=params(),
        cost_estimate=cost(1e11, 1e9),
    )(mine, swap, across)


def fold_kernel(near, arrived, out, total):
    total[...] = (near[...] + arrived[...].astype(jnp.float32)).astype(jnp.bfloat16)
    part = out.shape[2]
    for index in range(out.shape[0]):
        out[index] = total[:, index * part : (index + 1) * part]


def fold(count, near, arrived):
    rows, width = near.shape
    return pl.pallas_call(
        fold_kernel,
        in_specs=[WHOLE] * 2,
        out_specs=WHOLE,
        out_shape=jax.ShapeDtypeStruct((count, rows, width // count), jnp.bfloat16),
        scratch_shapes=[pltpu.VMEM((rows, width), jnp.bfloat16)],
        compiler_params=params(),
        cost_estimate=cost(2e6, 4e6),
    )(near, arrived)


def sum_kernel(parts, out):
    total = parts[0].astype(jnp.float32)
    for index in range(1, parts.shape[0]):
        total = total + parts[index].astype(jnp.float32)
    out[...] = total.astype(jnp.bfloat16)


def sum_parts(parts):
    return pl.pallas_call(
        sum_kernel,
        in_specs=[WHOLE],
        out_specs=WHOLE,
        out_shape=jax.ShapeDtypeStruct(parts.shape[1:], jnp.bfloat16),
        compiler_params=params(),
        cost_estimate=cost(4e5, 8e5),
    )(parts)


def body(hidden, head_weight, teacher_logits, teacher_ids):
    seq_count = lax.axis_size("seq")
    vocab_count = lax.axis_size("vocab")
    owners = seq_count * vocab_count
    vocab_rows, width = head_weight.shape
    tok_rows, feat_part = hidden.shape
    seq_index = lax.axis_index("seq")
    pos = jnp.stack([seq_index // 2, seq_index % 2]).astype(jnp.int32)
    ring = [(i, (i + 2 - 4 * (i % 2)) % seq_count) for i in range(seq_count)]
    cross = [(i, (i + 2 - 4 * (i % 2)) % seq_count ^ 1) for i in range(seq_count)]
    twin = [(i, i ^ 1) for i in range(seq_count)]

    def move(x, perm):
        return lax.ppermute(x, "seq", perm)

    def after(x, *before):
        return lax.optimization_barrier((x, before))[0]

    f32 = jnp.float32
    bf16 = jnp.bfloat16

    hidden, pos = lax.optimization_barrier((hidden, pos))
    spread = copies_of(hidden, vocab_count)
    spread = lax.all_to_all(spread, "vocab", split_axis=0, concat_axis=0, tiled=True)
    own = join_parts(spread)
    next1 = move(own, ring)
    own2 = move(own, twin)
    next2 = move(own2, ring)
    teacher_logits, own2 = lax.optimization_barrier((teacher_logits, own2))
    teach = teacher_rows(owners, vocab_rows, teacher_logits, teacher_ids)
    got = lax.all_to_all(teach, BOTH, split_axis=0, concat_axis=0, tiled=True)
    far = move(next1, ring)
    near_blocks = (own, own2, next1, next2)
    weight, logits, target, near_rows = first_logits(pos, got, head_weight, near_blocks)
    back = (move(next1, twin), move(after(next2, got), twin))
    far = after(far, logits)
    early = near_stats(pos, after(logits, back[1]), target)
    last, send, last_rows = last_logits(pos, weight, target, early, (*back, far, move(far, twin)))
    stats = lax.all_to_all(send, BOTH, split_axis=0, concat_axis=0, tiled=True)

    far_mine, far_other, grad_far, lse, loss = far_grad(pos, stats, last, target, weight)
    far_swap = move(far_other, twin)
    wide, first_left, second_left = near_grads(pos, logits, last, target, lse, grad_far)
    first_mine, first_other = near_grad(first_left, weight)
    first_swap = move(first_other, twin)
    far_sum = (far_mine + far_swap.astype(f32)).astype(bf16)
    passed = move(far_sum, ring)
    first_sum = (first_mine + first_swap.astype(f32)).astype(bf16)
    second_left = after(second_left, far_sum, first_sum)
    second_mine, second_other = near_grad(second_left, weight)
    second_swap = move(second_other, twin)
    first = move(first_sum, cross)
    passed = widen(after(passed, first_sum))
    second_sum = second_mine[:tok_rows] + second_swap[:tok_rows].astype(f32)
    second_sum = (second_sum + passed).astype(bf16)
    second = move(second_sum, ring)
    rows = teacher_logits.shape[0]
    loss = after(loss, second_sum)
    cross_entropy, entropy = loss[0, :rows], loss[1, :rows]
    wide = after(wide, second_sum, cross_entropy, entropy)
    grad_weight = weight_grad(wide, near_rows, last_rows)
    first = after(first, grad_weight)
    gathered = gather_own(second_mine, second_swap, first)
    second, gathered = lax.optimization_barrier((second, gathered))
    parts = fold(vocab_count, gathered, second)
    parts = lax.all_to_all(parts, "vocab", split_axis=0, concat_axis=0, tiled=True)
    grad_hidden = sum_parts(parts)
    return cross_entropy, entropy, grad_hidden, grad_weight


def solution(mesh):
    placed = (
        P("seq", "vocab"),
        P(("seq", "vocab"), None),
        P(("seq", "vocab"), None),
        P(("seq", "vocab"), None),
    )
    return jax.shard_map(
        body,
        mesh=mesh,
        in_specs=placed,
        out_specs=(
            P(("seq", "vocab")),
            P(("seq", "vocab")),
            P("seq", "vocab"),
            P(("seq", "vocab"), None),
        ),
        check_vma=False,
    )
```
